256 devices in a mesh: dp: 16 (over x_hi, y, core), tensor: 16 (over x_lo, z).
Axes of the slice: x: 4 (x_hi: 2, x_lo: 2; x = x_hi * 2 + x_lo), y: 4, z: 8, core: 2. Of those that a mesh axis runs over, the one named last changes fastest.
Arguments:
- tokens: bfloat16 [4096, 4096], P(('dp', 'tensor')), may hold values from -24 to 24
- gate_weight: bfloat16 [4096, 14336], P('dp', 'tensor'), may hold values from -0.09375 to 0.09375
- up_weight: bfloat16 [4096, 14336], P('dp', 'tensor'), may hold values from -0.09375 to 0.09375
- hidden_cotangent: bfloat16 [4096, 14336], P('dp', 'tensor'), may hold values from -1.5 to 1.5
Outputs:
- hidden: bfloat16 [4096, 14336], P('dp', 'tensor')
- grad_tokens: bfloat16 [4096, 4096], P(('dp', 'tensor'))
- grad_gate: bfloat16 [4096, 14336], P('dp', 'tensor')
- grad_up: bfloat16 [4096, 14336], P('dp', 'tensor')
The draws below stay inside these ranges and needn't reach their ends.
All inputs are finite; a program needn't handle non-finite values.
Results may differ from the reference program's by a relative error of at most 0.023.
Values may be sent and summed in bfloat16 or wider, within the bound.
A program may use at most 64 MiB of HBM per device.

```python
import jax
import jax.numpy as jnp
from jax import lax

D = 4096
GROUP_TOK = 256
FF = 14336
TOKENS = 4096
N_DP = 16


def with_spikes(result, key, source, target, parts, factor):
    owner, partner = [(jnp.arange(result.shape[dim]) // (result.shape[dim] // parts)).reshape([-1 if axis == dim else 1 for axis in range(result.ndim)]) for dim in (source, target)]
    chosen = jax.random.permutation(key, parts)[partner]
    strong = (owner == chosen) | (owner == (partner + parts // 2) % parts)
    return jnp.where(strong, factor * result, result)


def levels(key, shape, shards, least, largest):
    def one(axis_at, blocks):
        steps = jax.random.uniform(jax.random.fold_in(jax.random.fold_in(key, 6), axis_at), (blocks,), jnp.float32, least / len(shards), largest / len(shards))
        return jnp.repeat(jnp.exp(steps), shape[axis_at] // blocks).reshape((-1,) + (1,) * (len(shape) - axis_at - 1))

    loudness = one(*shards[0])
    for cut in shards[1:]:
        loudness = loudness * one(*cut)
    return loudness


def noise(rng, dims, spread, most, split=(), held_as=jnp.bfloat16):
    values = spread * jax.random.normal(rng, dims, jnp.float32)
    if split:
        values = values * levels(rng, dims, split, -0.22, 0.18)
    return jnp.clip(values, -most, most).astype(held_as)


def bell_draw_with(key, dims, spread, bound, cuts, heavy, kind=jnp.bfloat16):
    result = spread * jax.random.normal(key, dims, jnp.float32)
    if cuts:
        result = result * levels(key, dims, cuts, -0.22, 0.18)
    return jnp.clip(with_spikes(result, jax.random.fold_in(key, 3), *heavy), -bound, bound).astype(kind)


def setup_inputs(seed: int = 0) -> dict:
    key_of = jax.random.split(jax.random.key(seed), 5)
    tokens = bell_draw_with(key_of[0], (TOKENS, D), 1.0, 24.0, ((0, 256),), (0, 1, 256, 6.0))
    gate_weight = noise(key_of[1], (D, FF), D ** -0.5, 0.09375, ((0, 16), (1, 16)))
    up_weight = noise(key_of[2], (D, FF), D ** -0.5, 0.09375, ((0, 16), (1, 16)))
    hidden_cotangent = noise(key_of[3], (TOKENS, FF), 0.25, 1.5, ((0, 16), (1, 16)))
    return {"tokens": tokens, "gate_weight": gate_weight, "up_weight": up_weight, "hidden_cotangent": hidden_cotangent}


def swiglu_parts(gate_pre, up_pre, cotangent):
    sigmoid_val = jax.nn.sigmoid(gate_pre)
    activation = gate_pre * sigmoid_val
    hidden = (activation * up_pre).astype(jnp.bfloat16)
    upstream = cotangent.astype(jnp.float32)
    slope = sigmoid_val * (1.0 + gate_pre * (1.0 - sigmoid_val))
    grad_gate_pre = (upstream * up_pre * slope).astype(jnp.bfloat16)
    grad_up_pre = (upstream * activation).astype(jnp.bfloat16)
    return hidden, grad_gate_pre, grad_up_pre


def reference(tokens, gate_weight, up_weight, hidden_cotangent):
    gate_pre = jnp.dot(tokens, gate_weight, preferred_element_type=jnp.float32)
    up_pre = jnp.dot(tokens, up_weight, preferred_element_type=jnp.float32)
    hidden, grad_gate_pre, grad_up_pre = swiglu_parts(gate_pre, up_pre, hidden_cotangent)
    input_sum = jnp.dot(grad_gate_pre, gate_weight.T, preferred_element_type=jnp.float32)
    input_sum = input_sum + jnp.dot(grad_up_pre, up_weight.T, preferred_element_type=jnp.float32)
    grad_tokens = input_sum.astype(jnp.bfloat16)
    joined = jnp.concatenate([grad_gate_pre, grad_up_pre], axis=1)

    def add_group(carry, group_index):
        first_row = (group_index * GROUP_TOK).astype(jnp.int32)
        rows_part = lax.dynamic_slice_in_dim(tokens, first_row, GROUP_TOK, 0)
        grads_part = lax.dynamic_slice_in_dim(joined, first_row, GROUP_TOK, 0)
        term = jnp.dot(rows_part.T, grads_part, preferred_element_type=jnp.float32)
        term = lax.optimization_barrier(term.astype(jnp.bfloat16)).astype(jnp.float32)
        return carry + term, None

    total, _ = lax.scan(add_group, jnp.zeros((D, 2 * FF), jnp.float32), jnp.arange(N_DP, dtype=jnp.int32))
    grad_gate = total[:, :FF].astype(jnp.bfloat16)
    grad_up = total[:, FF:].astype(jnp.bfloat16)
    return hidden, grad_tokens, grad_gate, grad_up
```

```python
import jax
import jax.numpy as jnp
from jax import lax
from jax.sharding import Mesh
from jax.sharding import PartitionSpec as P

SPLIT = ("xh", "c")
TENSOR = ("xl", "z")
DP = ("xh", "y", "c")
ROWS = P((*DP, *TENSOR), None)
BLOCK = P(DP, TENSOR)


def swiglu_parts(gate_pre, up_pre, cotangent):
    sigmoid_val = jax.nn.sigmoid(gate_pre)
    activation = gate_pre * sigmoid_val
    hidden = (activation * up_pre).astype(jnp.bfloat16)
    upstream = cotangent.astype(jnp.float32)
    slope = sigmoid_val * (1.0 + gate_pre * (1.0 - sigmoid_val))
    grad_gate_pre = (upstream * up_pre * slope).astype(jnp.bfloat16)
    grad_up_pre = (upstream * activation).astype(jnp.bfloat16)
    return (hidden, grad_gate_pre, grad_up_pre)


def body(tokens, gate_weight, up_weight, cotangent):
    rows, model = tokens.shape
    depth, width = gate_weight.shape
    nx, ny, nc = (lax.axis_size(a) for a in DP)
    nt = lax.axis_size(TENSOR)
    cut = tokens.reshape(rows, nx, ny, nc, depth).transpose(1, 3, 0, 2, 4)
    cut = cut.reshape(nx * nc, rows, ny * depth)
    cut = lax.all_to_all(cut, SPLIT, 0, 0, tiled=True)
    mine = lax.all_gather(cut, TENSOR, axis=1, tiled=True)
    mine = mine.reshape(nx * nc * nt * rows, ny * depth)
    weights = lax.all_gather(
        jnp.concatenate([gate_weight, up_weight], axis=1), "y", axis=0, tiled=True
    )
    part = jnp.dot(mine, weights, preferred_element_type=jnp.float32).astype(jnp.bfloat16)
    pre = lax.psum_scatter(part, SPLIT, scatter_dimension=0, tiled=True).astype(jnp.float32)
    hidden, grad_gate_pre, grad_up_pre = swiglu_parts(pre[:, :width], pre[:, width:], cotangent)
    grads = lax.all_gather(
        jnp.concatenate([grad_gate_pre, grad_up_pre], axis=1), SPLIT, axis=0, tiled=True
    )
    back = lax.dot_general(
        grads, weights, (((1,), (1,)), ((), ())), preferred_element_type=jnp.float32
    ).astype(jnp.bfloat16)
    nl, nz = (lax.axis_size(a) for a in TENSOR)
    back = back.reshape(nx * nc, nl, nz, rows, ny * depth).transpose(2, 1, 0, 3, 4)
    back = lax.psum_scatter(back, "z", scatter_dimension=0, tiled=True)[0]
    back = lax.psum_scatter(back, "xl", scatter_dimension=0, tiled=True)[0]
    back = lax.all_to_all(back, SPLIT, 0, 0, tiled=True)
    back = back.reshape(nx, nc, rows, ny, depth).transpose(2, 0, 3, 1, 4).reshape(rows, model)
    total = lax.dot_general(
        mine, grads, (((0,), (0,)), ((), ())), preferred_element_type=jnp.float32
    ).astype(jnp.bfloat16)
    total = lax.psum_scatter(total, "y", scatter_dimension=0, tiled=True)
    return (hidden, back, total[:, :width], total[:, width:])


def solution(mesh):
    torus = Mesh(mesh.devices.reshape(2, 4, 2, 2, 8), (*DP, *TENSOR))
    specs = (ROWS, BLOCK, BLOCK, BLOCK)
    outs = (BLOCK, ROWS, BLOCK, BLOCK)
    return jax.shard_map(body, mesh=torus, in_specs=specs, out_specs=outs, check_vma=False)
```

```python
import functools

import jax
import jax.numpy as jnp
from jax import lax
from jax.experimental import pallas as pl
from jax.experimental.pallas import tpu as pltpu
from jax.sharding import Mesh
from jax.sharding import PartitionSpec as P

SPLIT = ("xh", "c")
TENSOR = ("xl", "z")
DP = ("xh", "y", "c")
ROWS = P((*DP, *TENSOR), None)
BLOCK = P(DP, TENSOR)
MESH = pl.DeviceIdType.MESH
F32 = jnp.float32
BF16 = jnp.bfloat16
CHUNKS = ((0, 512), (512, 384))
NZ = 8
TILE = 256
CUBE = tuple((a, b, d) for a in range(2) for b in range(2) for d in range(2))
STEPS = 4


def dot(a, b):
    return jnp.dot(a, b, preferred_element_type=F32)


def dot_nt(a, b):
    return lax.dot_general(a, b, (((1,), (1,)), ((), ())), preferred_element_type=F32)


def kernel(
    tokens, gate, up, cot, hidden, rows_out, grad_gate, grad_up,
    x, xt, w0, w1, pc0, pc1, rc0, rc1, px0, px1, rx0, rx1, po0, po1, g0, g1, dw0, dw1,
    ry0, ry1, qy0, qy1, dx, zs, zr, ts, tr, loc, cs, cr, zgs, zgr, ws, wr, ms, mr, ys, yr, zrs, zrr, fs, fr,
):
    xh, y, c, xl, z = (lax.axis_index(a) for a in ("xh", "y", "c", "xl", "z"))
    yp, ym, y2 = lax.rem(y + 1, 4), lax.rem(y + 3, 4), lax.rem(y + 2, 4)
    zp, zm = lax.rem(z + 1, NZ), lax.rem(z + NZ - 1, NZ)
    W, PC, RC, PX, RX, PO = (w0, w1), (pc0, pc1), (rc0, rc1), (px0, px1), (rx0, rx1), (po0, po1)
    G, DW, RY, QY = (g0, g1), (dw0, dw1), (ry0, ry1), (qy0, qy1)
    both = range(len(CHUNKS))
    sent = []

    def go(src, dst, send, recv, to):
        copy = pltpu.make_async_remote_copy(
            src_ref=src, dst_ref=dst, send_sem=send, recv_sem=recv,
            device_id=to, device_id_type=MESH,
        )
        copy.start()
        sent.append(copy)
        return copy

    def flip(a, b, d):
        return (
            1 - xh if a else xh,
            1 - c if b else c,
            1 - xl if d else xl,
        )

    def cube_id(a, b, d):
        px, pc, plo = flip(a, b, d)
        return {"xh": px, "c": pc, "xl": plo}

    local = []
    for k, (at, wide) in enumerate(CHUNKS):
        local.append(pltpu.make_async_copy(gate.at[:, pl.ds(at, wide)], W[k].at[y, :, pl.ds(0, wide)], loc.at[2 * k]))
        local.append(pltpu.make_async_copy(up.at[:, pl.ds(at, wide)], W[k].at[y, :, pl.ds(wide, wide)], loc.at[2 * k + 1]))
    own = pltpu.make_async_copy(tokens.at[2 * xh + c], x.at[2 * xh + c, xl, z], loc.at[4])
    for copy in (own, *local):
        copy.start()

    barrier = pltpu.get_barrier_semaphore()
    peers = [{"y": yp}, {"y": ym}, {"z": zp}, {"z": zm}] + [cube_id(*k) for k in CUBE[1:]]
    for peer in peers:
        pl.semaphore_signal(barrier, inc=1, device_id=peer, device_id_type=MESH)
    pl.semaphore_wait(barrier, len(peers))

    cube = []
    for k, key in enumerate(CUBE):
        if k:
            a, b, _ = flip(*key)
            cube.append(go(tokens.at[2 * a + b], x.at[2 * xh + c, xl, z], cs.at[k - 1], cr.at[k - 1], cube_id(*key)))

    def send_weights(k):
        return (
            go(W[k].at[y], W[k].at[y], ws.at[k, 0], wr.at[k, 0], {"y": yp}),
            go(W[k].at[y], W[k].at[y], ws.at[k, 1], wr.at[k, 1], {"y": ym}),
        )

    def relay_weights(k):
        return (
            go(W[k].at[ym, pl.ds(0, 128)], W[k].at[ym, pl.ds(0, 128)], ws.at[k, 2], wr.at[k, 2], {"y": yp}),
            go(W[k].at[yp, pl.ds(128, 128)], W[k].at[yp, pl.ds(128, 128)], ws.at[k, 3], wr.at[k, 3], {"y": ym}),
        )

    for copy in local:
        copy.wait()
    first = send_weights(0)
    own.wait()
    for copy in cube:
        copy.wait_recv()

    def part(at, h):
        return x.at[pl.ds(2 * h, 2), :, at]

    def z_step(step):
        out = []
        for h in range(2):
            if step < 3 or h == 0:
                at = lax.rem(z + NZ - step, NZ)
                out.append(go(part(at, h), part(at, h), zgs.at[step, h, 0], zgr.at[step, h, 0], {"z": zp}))
            if step < 3 or h == 1:
                at = lax.rem(z + step, NZ)
                out.append(go(part(at, h), part(at, h), zgs.at[step, h, 1], zgr.at[step, h, 1], {"z": zm}))
        return out

    def arrived(copies):
        for copy in copies:
            copy.wait_recv()

    moving = z_step(0)
    arrived(moving)
    moving = z_step(1)
    arrived(first)
    relay0 = relay_weights(0)
    second = send_weights(1)
    arrived(moving)
    moving = z_step(2)
    arrived(moving)
    moving = z_step(3)
    arrived(second)
    relay1 = relay_weights(1)
    arrived(moving)
    arrived(relay0)

    def block(ref, at):
        return ref[at].reshape(256, 1024)

    def columns(j):
        return pl.ds(pl.multiple_of(j * TILE, TILE), TILE)

    def partial(k, at, store):
        def step(j, _):
            cols = columns(j)
            store(cols, dot(block(x, at), W[k][:, :, cols].reshape(1024, TILE)))
            return 0
        lax.fori_loop(0, 2 * CHUNKS[k][1] // TILE, step, 0)

    def forward(k):
        def to_core(at):
            def store(cols, value):
                PC[k][at, :, cols] = value.astype(BF16)
            return store

        def to_x(cols, value):
            PX[k][:, cols] = (value + RC[k][1 - xh, :, cols].astype(F32)).astype(BF16)

        def to_own(cols, value):
            PO[k][:, cols] = value

        core = {"c": 1 - c}
        partial(k, 2 * (1 - xh) + 1 - c, to_core(1 - xh))
        far = go(PC[k].at[1 - xh], RC[k].at[1 - xh], ms.at[k, 0], mr.at[k, 0], core)
        partial(k, 2 * xh + 1 - c, to_core(xh))
        near = go(PC[k].at[xh], RC[k].at[xh], ms.at[k, 1], mr.at[k, 1], core)
        far.wait_recv()
        partial(k, 2 * (1 - xh) + c, to_x)
        across = go(PX[k], RX[k], ms.at[k, 2], mr.at[k, 2], {"xh": 1 - xh})
        partial(k, 2 * xh + c, to_own)
        return near, across

    def middle(k):
        at, wide = CHUNKS[k]
        me = 2 * xh + c

        def step(i, _):
            rows = pl.ds(pl.multiple_of(i * 16, 16), 16)
            pre = PO[k][rows, :] + RC[k][xh, rows, :].astype(F32) + RX[k][rows, :].astype(F32)
            gate_pre, up_pre = pre[:, :wide], pre[:, wide:]
            sigma = jax.nn.sigmoid(gate_pre)
            activation = gate_pre * sigma
            upstream = cot[rows, pl.ds(at, wide)].astype(F32)
            slope = sigma * (1.0 + gate_pre * (1.0 - sigma))
            hidden[rows, pl.ds(at, wide)] = (activation * up_pre).astype(BF16)
            G[k][me, rows, pl.ds(0, wide)] = (upstream * up_pre * slope).astype(BF16)
            G[k][me, rows, pl.ds(wide, wide)] = (upstream * activation).astype(BF16)
            return 0

        lax.fori_loop(0, 16, step, 0)
        return (
            go(G[k].at[me], G[k].at[me], ms.at[k, 3], mr.at[k, 3], {"xh": 1 - xh}),
            go(G[k].at[me], G[k].at[me], ms.at[k, 4], mr.at[k, 4], {"c": 1 - c}),
        )

    def pass_on(k):
        at = 2 * (1 - xh) + c
        return go(G[k].at[at], G[k].at[at], ms.at[k, 5], mr.at[k, 5], {"c": 1 - c})

    near0, across0 = forward(0)
    arrived(relay1)
    near1, across1 = forward(1)

    def turn(i, _):
        at, j = i // 4, lax.rem(i, 4)
        cols = columns(j)
        xt[cols, columns(at)] = x[at, :, :, :, cols].reshape(256, TILE).T
        return 0

    lax.fori_loop(0, 16, turn, 0)

    near0.wait_recv()
    across0.wait_recv()
    xg0, cg0 = middle(0)
    near1.wait_recv()
    across1.wait_recv()
    xg1, cg1 = middle(1)
    cg0.wait_recv()
    cg1.wait_recv()

    def back(group):
        def step(i, _):
            at, j = 2 * group + i // 4, lax.rem(i, 4)
            total = dot_nt(G[0][at], W[0][j]) + dot_nt(G[1][at], W[1][j])
            dx[at, :, :, :, columns(j)] = total.reshape(2, NZ, 16, TILE)
            return 0
        lax.fori_loop(0, 8, step, 0)

    def z_sum(h, group, step, came):
        out = []
        for way in range(2):
            to = {"z": zm if way else zp}
            far = STEPS - step
            dest = lax.rem(z + (NZ - far if way else far), NZ)
            if step == 0:
                zs[h, way, 0, 0] = dx[2 * group + way, :, dest].astype(BF16)
                out.append(go(zs.at[h, way, 0, 0], zr.at[h, way, 0, 0], zrs.at[h, 0, way], zrr.at[h, 0, way], to))
                continue
            came[way].wait_recv()
            if step == 1:
                zs[h, way, 1, way] = (dx[2 * group + way, :, dest] + zr[h, way, 0, 0].astype(F32)).astype(BF16)
                zs[h, way, 1, 1 - way] = dx[2 * group + 1 - way, :, dest].astype(BF16)
            else:
                for b in range(2):
                    zs[h, way, step, b] = (dx[2 * group + b, :, dest] + zr[h, way, step - 1, b].astype(F32)).astype(BF16)
            out.append(go(zs.at[h, way, step], zr.at[h, way, step], zrs.at[h, step, way], zrr.at[h, step, way], to))
        return out

    def z_last(h, group, came):
        arrived(came)
        out = []
        for b in range(2):
            total = dx[2 * group + b, :, z] + zr[h, 0, 3, b].astype(F32) + zr[h, 1, 3, b].astype(F32)
            ts[group, b] = total.astype(BF16)
        for k, key in enumerate(CUBE):
            a, b, d = flip(*key)
            if key[0] == h and k:
                out.append(go(ts.at[a, b, d], tr.at[xh, c, xl], fs.at[k - 1], fr.at[k - 1], cube_id(*key)))
        if h == 0:
            keep = pltpu.make_async_copy(ts.at[xh, c, xl], tr.at[xh, c, xl], loc.at[5])
            keep.start()
            keep.wait()
        return out

    back(xh)
    zc = z_sum(0, xh, 0, None)

    def weight_grad(k, at):
        def step(j, _):
            cols = columns(j)
            rows = columns(at)
            DW[k][at, :, cols] = dot(xt[rows, :], G[k][:, :, cols].reshape(1024, TILE)).astype(BF16)
            return 0
        lax.fori_loop(0, 2 * CHUNKS[k][1] // TILE, step, 0)

    upper, lower = pl.ds(0, 128), pl.ds(128, 128)

    def sums_out(k):
        weight_grad(k, y2)
        a = go(DW[k].at[y2, upper], QY[k].at[0], ys.at[k, 0], yr.at[k, 0], {"y": yp})
        b = go(DW[k].at[y2, lower], QY[k].at[1], ys.at[k, 1], yr.at[k, 1], {"y": ym})
        weight_grad(k, yp)
        e = go(DW[k].at[yp, lower], RY[k].at[0, lower], ys.at[k, 2], yr.at[k, 2], {"y": yp})
        weight_grad(k, ym)
        f = go(DW[k].at[ym, upper], RY[k].at[1, upper], ys.at[k, 3], yr.at[k, 3], {"y": ym})
        weight_grad(k, y)
        return a, b, e, f

    def sums_on(k, a, b):
        a.wait_recv()
        DW[k][yp, upper] = (DW[k][yp, upper].astype(F32) + QY[k][0].astype(F32)).astype(BF16)
        e = go(DW[k].at[yp, upper], RY[k].at[0, upper], ys.at[k, 4], yr.at[k, 4], {"y": yp})
        b.wait_recv()
        DW[k][ym, lower] = (DW[k][ym, lower].astype(F32) + QY[k][1].astype(F32)).astype(BF16)
        f = go(DW[k].at[ym, lower], RY[k].at[1, lower], ys.at[k, 5], yr.at[k, 5], {"y": ym})
        return e, f

    def sums_in(k, copies):
        at, wide = CHUNKS[k]
        arrived(copies)

        def step(i, _):
            rows = pl.ds(pl.multiple_of(i * 32, 32), 32)
            total = DW[k][y, rows].astype(F32) + RY[k][0, rows].astype(F32) + RY[k][1, rows].astype(F32)
            total = total.astype(BF16)
            grad_gate[rows, pl.ds(at, wide)] = total[:, :wide]
            grad_up[rows, pl.ds(at, wide)] = total[:, wide:]
            return 0

        lax.fori_loop(0, 8, step, 0)

    xg0.wait_recv()
    pass0 = pass_on(0)
    zc = z_sum(0, xh, 1, zc)
    pass0.wait_recv()
    y0 = sums_out(0)
    zc = z_sum(0, xh, 2, zc)
    xg1.wait_recv()
    pass1 = pass_on(1)
    zc = z_sum(0, xh, 3, zc)
    pass1.wait_recv()
    back(1 - xh)
    zd = z_sum(1, 1 - xh, 0, None)
    y0n = sums_on(0, y0[0], y0[1])
    y1 = sums_out(1)
    zd = z_sum(1, 1 - xh, 1, zd)
    end0 = z_last(0, xh, zc)
    zd = z_sum(1, 1 - xh, 2, zd)
    y1n = sums_on(1, y1[0], y1[1])
    zd = z_sum(1, 1 - xh, 3, zd)
    sums_in(0, (y0[2], y0[3], *y0n))
    end1 = z_last(1, 1 - xh, zd)
    sums_in(1, (y1[2], y1[3], *y1n))
    arrived(end0)
    arrived(end1)
    for a in range(2):
        for b in range(2):
            rows_out[2 * a + b] = (tr[a, b, 0].astype(F32) + tr[a, b, 1].astype(F32)).astype(BF16)
    for copy in sent:
        copy.wait_send()


def body(tokens, gate_weight, up_weight, cotangent):
    rows, model = tokens.shape
    depth, width = gate_weight.shape
    nx, ny, nc = (lax.axis_size(a) for a in DP)
    cut = tokens.reshape(rows, nx, ny, nc, depth).transpose(1, 3, 0, 2, 4)
    cut = cut.reshape(nx * nc, rows, ny * depth)
    wides = [2 * wide for _, wide in CHUNKS]
    dma = pltpu.SemaphoreType.DMA

    def per_chunk(*lead, dtype=BF16):
        return [pltpu.VMEM((*lead, wide), dtype) for wide in wides]

    vmem = pl.BlockSpec(memory_space=pltpu.VMEM)
    grid = pl.BlockSpec(memory_space=pl.ANY)
    tile = jax.ShapeDtypeStruct((depth, width), BF16)
    hidden, back, grad_gate, grad_up = pl.pallas_call(
        kernel,
        out_shape=(tile, jax.ShapeDtypeStruct((nx * nc, rows, ny * depth), BF16), tile, tile),
        in_specs=[vmem, grid, grid, vmem],
        out_specs=(vmem, vmem, vmem, vmem),
        scratch_shapes=[
            pltpu.VMEM((4, 2, NZ, 16, 1024), BF16),
            pltpu.VMEM((1024, 1024), BF16),
            *per_chunk(4, 256),
            *per_chunk(2, 256),
            *per_chunk(2, 256),
            *per_chunk(256),
            *per_chunk(256),
            *per_chunk(256, dtype=F32),
            *per_chunk(4, 256),
            *per_chunk(4, 256),
            *per_chunk(2, 256),
            *per_chunk(2, 128),
            pltpu.VMEM((4, 2, NZ, 16, 1024), F32),
            pltpu.VMEM((2, 2, STEPS, 2, 2, 16, 1024), BF16),
            pltpu.VMEM((2, 2, STEPS, 2, 2, 16, 1024), BF16),
            pltpu.VMEM((2, 2, 2, 16, 1024), BF16),
            pltpu.VMEM((2, 2, 2, 16, 1024), BF16),
            dma((6,)), dma((7,)), dma((7,)),
            dma((4, 2, 2)), dma((4, 2, 2)),
            dma((2, 4)), dma((2, 4)),
            dma((2, 6)), dma((2, 6)),
            dma((2, 6)), dma((2, 6)),
            dma((2, STEPS, 2)), dma((2, STEPS, 2)),
            dma((7,)), dma((7,)),
        ],
        compiler_params=pltpu.CompilerParams(
            collective_id=0, has_side_effects=True, vmem_limit_bytes=56 * 2**20
        ),
        name="swiglu",
    )(cut, gate_weight, up_weight, cotangent)
    back = back.reshape(nx, nc, rows, ny, depth).transpose(2, 0, 3, 1, 4).reshape(rows, model)
    return (hidden, back, grad_gate, grad_up)


def solution(mesh):
    torus = Mesh(mesh.devices.reshape(2, 4, 2, 2, 8), (*DP, *TENSOR))
    specs = (ROWS, BLOCK, BLOCK, BLOCK)
    outs = (BLOCK, ROWS, BLOCK, BLOCK)
    return jax.shard_map(body, mesh=torus, in_specs=specs, out_specs=outs, check_vma=False)
```

```python
import functools

import jax
import jax.numpy as jnp
from jax import lax
from jax.experimental import pallas as pl
from jax.experimental.pallas import tpu as pltpu
from jax.sharding import Mesh
from jax.sharding import PartitionSpec as P

SPLIT = ("xh", "c")
TENSOR = ("xl", "z")
DP = ("xh", "y", "c")
ROWS = P((*DP, *TENSOR), None)
BLOCK = P(DP, TENSOR)
MESH = pl.DeviceIdType.MESH
F32 = jnp.float32
BF16 = jnp.bfloat16
CHUNKS = ((0, 256), (256, 384), (640, 256))
NZ = 8
TILE = 256
OFFSETS = (0, 1, -1, 2, -2, 3, -3, 4)
CUBE = tuple((a, b, d) for a in range(2) for b in range(2) for d in range(2))
STEPS = 4


def dot(a, b):
    return jnp.dot(a, b, preferred_element_type=F32)


def dot_nt(a, b):
    return lax.dot_general(a, b, (((1,), (1,)), ((), ())), preferred_element_type=F32)


def kernel(tokens, gate, up, cot, hidden, rows_out, grad_gate, grad_up, *scratch):
    n = len(CHUNKS)
    W, PC, RC, PX, RX, PO, G, DW, RY, QY = (scratch[i * n : (i + 1) * n] for i in range(10))
    (
        x, xt, stage, dx, zs, zr, ts, tr,
        loc, cs, cr, zgs, zgr, ws, wr, ms, mr, ys, yr, zrs, zrr, fs, fr,
    ) = scratch[10 * n :]
    xh, y, c, xl, z = (lax.axis_index(a) for a in ("xh", "y", "c", "xl", "z"))
    yp, ym, y2 = lax.rem(y + 1, 4), lax.rem(y + 3, 4), lax.rem(y + 2, 4)
    zp, zm = lax.rem(z + 1, NZ), lax.rem(z + NZ - 1, NZ)
    core, across = {"c": 1 - c}, {"xh": 1 - xh}
    sent = []

    def go(src, dst, send, recv, to):
        copy = pltpu.make_async_remote_copy(
            src_ref=src, dst_ref=dst, send_sem=send, recv_sem=recv,
            device_id=to, device_id_type=MESH,
        )
        copy.start()
        sent.append(copy)
        return copy

    def arrived(copies):
        for copy in copies:
            copy.wait_recv()

    def flip(a, b, d):
        return (1 - xh if a else xh, 1 - c if b else c, 1 - xl if d else xl)

    def cube_id(a, b, d):
        px, pc, plo = flip(a, b, d)
        return {"xh": px, "c": pc, "xl": plo}

    def slot(offset):
        return divmod(OFFSETS.index(offset if offset != -4 else 4), 4)

    def half(hs):
        return pl.ds(hs[0], len(hs))

    local = []
    for k, (at, wide) in enumerate(CHUNKS):
        for i, ref in enumerate((gate, up)):
            copy = pltpu.make_async_copy(
                ref.at[:, pl.ds(at, wide)], W[k].at[y, :, pl.ds(i * wide, wide)], loc.at[2 * k + i]
            )
            copy.start()
            local.append(copy)
    for a in range(2):
        for b in range(2):
            for i in range(4):
                at = ((a * 4 + i) * 2 + b) * 256
                stage[2 * a + b, :, i * 256 : (i + 1) * 256] = tokens[:, at : at + 256]
    x[0, c, xh, xl, 0] = stage[2 * xh + c]

    barrier = pltpu.get_barrier_semaphore()
    peers = [{"y": yp}, {"y": ym}, {"z": zp}, {"z": zm}] + [cube_id(*k) for k in CUBE[1:]]
    for peer in peers:
        pl.semaphore_signal(barrier, inc=1, device_id=peer, device_id_type=MESH)
    pl.semaphore_wait(barrier, len(peers))

    cube = [None]
    for k, key in enumerate(CUBE):
        if k:
            a, b, _ = flip(*key)
            cube.append(go(stage.at[2 * a + b], x.at[0, c, xh, xl, 0], cs.at[k - 1], cr.at[k - 1], cube_id(*key)))

    def send_weights(k):
        return (
            go(W[k].at[y], W[k].at[y], ws.at[k, 0], wr.at[k, 0], {"y": yp}),
            go(W[k].at[y], W[k].at[y], ws.at[k, 1], wr.at[k, 1], {"y": ym}),
        )

    def relay_weights(k):
        return (
            go(W[k].at[ym, pl.ds(0, 128)], W[k].at[ym, pl.ds(0, 128)], ws.at[k, 2], wr.at[k, 2], {"y": yp}),
            go(W[k].at[yp, pl.ds(128, 128)], W[k].at[yp, pl.ds(128, 128)], ws.at[k, 3], wr.at[k, 3], {"y": ym}),
        )

    for copy in local:
        copy.wait()
    direct = [send_weights(0), send_weights(1)]
    relay = []

    moving = {}

    def z_step(step):
        for i in range(4):
            if step == 0:
                arrived(cube[max(1, 2 * i) : 2 * i + 2])
            px, pc, _ = flip(i // 2, i % 2, 0)
            for way in range(2):
                if (step - 1, i, way) in moving:
                    moving[step - 1, i, way].wait_recv()
                if step == 3 and i // 2 != way:
                    continue
                sign = 1 if way else -1
                (h, at), (h2, to) = slot(sign * step), slot(sign * (step + 1))
                moving[step, i, way] = go(
                    x.at[h, pc, px, :, at], x.at[h2, pc, px, :, to],
                    zgs.at[step, i, way], zgr.at[step, i, way], {"z": zm if way else zp},
                )

    def columns(j):
        return pl.ds(pl.multiple_of(j * TILE, TILE), TILE)

    def matrix(ref, k):
        return ref[k][...].reshape(1024, 2 * CHUNKS[k][1])

    def forward(k, hs):
        sl, m, w = half(hs), len(hs), 2 * CHUNKS[k][1]
        value = dot(x[sl, 1 - c].reshape(256 * m, 1024), matrix(W, k))
        PC[k][sl] = value.astype(BF16).reshape(m, 2, 128, w)
        near = go(PC[k].at[sl], RC[k].at[sl], ms.at[k, hs[0]], mr.at[k, hs[0]], core)
        value = dot(x[sl, c].reshape(256 * m, 1024), matrix(W, k))
        PO[k][sl] = value.reshape(m, 2, 128, w)
        near.wait_recv()
        PX[k][sl] = (PO[k][sl, 1 - xh] + RC[k][sl, 1 - xh].astype(F32)).astype(BF16)

    def sums_across(k, hs):
        sl, i = half(hs), 2 + hs[0]
        return go(PX[k].at[sl], RX[k].at[sl], ms.at[k, i], mr.at[k, i], across)

    def grads_across(k, hs):
        part, i = G[k].at[half(hs), c, xh], 4 + hs[0]
        return go(part, part, ms.at[k, i], mr.at[k, i], across)

    def pass_on(k, hs):
        part, i = G[k].at[half(hs), c, 1 - xh], 7 + hs[0]
        return go(part, part, ms.at[k, i], mr.at[k, i], core)

    def middle(k):
        at, wide = CHUNKS[k]

        def step(i, _):
            h, j = i // 8, lax.rem(i, 8)
            rows = pl.ds(pl.multiple_of(j * 16, 16), 16)
            r = 4 * h + lax.rem(j, 4)
            there = lax.rem(z + NZ + (r + 1) // 2 * (2 * lax.rem(r, 2) - 1), NZ)
            place = pl.ds(pl.multiple_of((j // 4 * NZ + there) * 16, 16), 16)
            pre = PO[k][h, xh, rows, :] + RC[k][h, xh, rows, :].astype(F32) + RX[k][h, rows, :].astype(F32)
            gate_pre, up_pre = pre[:, :wide], pre[:, wide:]
            sigma = jax.nn.sigmoid(gate_pre)
            activation = gate_pre * sigma
            upstream = cot[place, pl.ds(at, wide)].astype(F32)
            slope = sigma * (1.0 + gate_pre * (1.0 - sigma))
            hidden[place, pl.ds(at, wide)] = (activation * up_pre).astype(BF16)
            G[k][h, c, xh, rows, pl.ds(0, wide)] = (upstream * up_pre * slope).astype(BF16)
            G[k][h, c, xh, rows, pl.ds(wide, wide)] = (upstream * activation).astype(BF16)
            return 0

        lax.fori_loop(0, 16, step, 0)
        part = G[k].at[:, c, xh]
        return go(part, part, ms.at[k, 6], mr.at[k, 6], core)

    def turn(i, _):
        at, j = i // 4, lax.rem(i, 4)
        cols = columns(j)
        xt[cols, columns(at)] = x[at // 2, lax.rem(at, 2), :, :, :, :, cols].reshape(256, TILE).T
        return 0

    def back(g, h, chunks, add):
        total = sum(
            dot_nt(G[k][h, :, g].reshape(256, 2 * CHUNKS[k][1]), matrix(W, k)) for k in chunks
        )
        total = total.reshape(2, 2, 4, 16, 1024)
        dx[h, :, g] = total + dx[h, :, g] if add else total

    flows = {}

    def z_sum(h, step):
        for b in range(2):
            gx, gc, _ = flip(h, b, 0)
            for way in range(2):
                if step == 0 and b != way:
                    continue
                far = STEPS - step
                side, at = slot(-far if way else far)
                value = dx[side, gc, gx, :, at]
                if (h, step - 1, way, b) in flows:
                    flows[h, step - 1, way, b].wait_recv()
                    value = value + zr[h, way, step - 1, b].astype(F32)
                zs[h, way, step, b] = value.astype(BF16)
                flows[h, step, way, b] = go(
                    zs.at[h, way, step, b], zr.at[h, way, step, b],
                    zrs.at[h, step, way, b], zrr.at[h, step, way, b], {"z": zm if way else zp},
                )

    def z_last(h):
        out = []
        for b in range(2):
            arrived((flows[h, 3, 0, b], flows[h, 3, 1, b]))
            gx, gc, _ = flip(h, b, 0)
            total = dx[0, gc, gx, :, 0] + zr[h, 0, 3, b].astype(F32) + zr[h, 1, 3, b].astype(F32)
            ts[gx, gc] = total.astype(BF16)
            for d in range(2):
                key = (h, b, d)
                k = CUBE.index(key)
                at = flip(*key)
                if k:
                    out.append(go(ts.at[at], tr.at[xh, c, xl], fs.at[k - 1], fr.at[k - 1], cube_id(*key)))
        if h == 0:
            tr[xh, c, xl] = ts[xh, c, xl]
        return out

    def weight_grad(k, at):
        DW[k][at] = dot(xt[columns(at), :], matrix(G, k)).astype(BF16)

    upper, lower = pl.ds(0, 128), pl.ds(128, 128)

    def sums_out(k):
        weight_grad(k, y2)
        a = go(DW[k].at[y2, upper], QY[k].at[0], ys.at[k, 0], yr.at[k, 0], {"y": yp})
        b = go(DW[k].at[y2, lower], QY[k].at[1], ys.at[k, 1], yr.at[k, 1], {"y": ym})
        weight_grad(k, yp)
        e = go(DW[k].at[yp, lower], RY[k].at[0, lower], ys.at[k, 2], yr.at[k, 2], {"y": yp})
        weight_grad(k, ym)
        f = go(DW[k].at[ym, upper], RY[k].at[1, upper], ys.at[k, 3], yr.at[k, 3], {"y": ym})
        weight_grad(k, y)
        return a, b, e, f

    def sums_on(k, a, b):
        a.wait_recv()
        DW[k][yp, upper] = (DW[k][yp, upper].astype(F32) + QY[k][0].astype(F32)).astype(BF16)
        e = go(DW[k].at[yp, upper], RY[k].at[0, upper], ys.at[k, 4], yr.at[k, 4], {"y": yp})
        b.wait_recv()
        DW[k][ym, lower] = (DW[k][ym, lower].astype(F32) + QY[k][1].astype(F32)).astype(BF16)
        f = go(DW[k].at[ym, lower], RY[k].at[1, lower], ys.at[k, 5], yr.at[k, 5], {"y": ym})
        return e, f

    def sums_in(k, copies):
        at, wide = CHUNKS[k]
        arrived(copies)

        def step(i, _):
            rows = pl.ds(pl.multiple_of(i * 32, 32), 32)
            total = DW[k][y, rows].astype(F32) + RY[k][0, rows].astype(F32) + RY[k][1, rows].astype(F32)
            total = total.astype(BF16)
            grad_gate[rows, pl.ds(at, wide)] = total[:, :wide]
            grad_up[rows, pl.ds(at, wide)] = total[:, wide:]
            return 0

        lax.fori_loop(0, 8, step, 0)

    z_step(0)
    z_step(1)
    arrived(direct[0])
    relay.append(relay_weights(0))
    z_step(2)
    arrived(relay[0])
    forward(0, (0,))
    a0 = sums_across(0, (0,))
    arrived(direct[1])
    relay.append(relay_weights(1))
    direct.append(send_weights(2))
    z_step(3)
    arrived([moving[key] for key in moving if key[0] == 3])
    forward(0, (1,))
    a0.wait_send()
    b0 = sums_across(0, (1,))
    lax.fori_loop(0, 8, turn, 0)
    arrived(relay[1])
    forward(1, (0, 1))
    b0.wait_send()
    s1 = sums_across(1, (0, 1))
    a0.wait_recv()
    b0.wait_recv()
    c0 = middle(0)
    arrived(direct[2])
    relay.append(relay_weights(2))
    lax.fori_loop(8, 16, turn, 0)
    arrived(relay[2])
    forward(2, (0, 1))
    s1.wait_send()
    g0 = grads_across(0, (0, 1))
    s1.wait_recv()
    c1 = middle(1)
    g0.wait_send()
    s2 = sums_across(2, (0, 1))
    g0.wait_recv()
    p0 = pass_on(0, (0, 1))
    arrived((c0, p0))
    y0 = sums_out(0)
    s2.wait_send()
    g1 = grads_across(1, (0, 1))
    s2.wait_recv()
    c2 = middle(2)
    arrived((c1, c2))
    back(xh, 1, (0, 1, 2), False)
    z_sum(0, 0)
    back(xh, 0, (0, 1, 2), False)
    y0n = sums_on(0, y0[0], y0[1])
    g1.wait_send()
    g2b = grads_across(2, (1,))
    z_sum(0, 1)
    g2b.wait_send()
    g2a = grads_across(2, (0,))
    g1.wait_recv()
    p1 = pass_on(1, (0, 1))
    z_sum(0, 2)
    p1.wait_recv()
    back(1 - xh, 1, (0, 1), False)
    g2b.wait_recv()
    p2b = pass_on(2, (1,))
    back(1 - xh, 0, (0, 1), False)
    p2b.wait_recv()
    back(1 - xh, 1, (2,), True)
    z_sum(1, 0)
    g2a.wait_recv()
    p2a = pass_on(2, (0,))
    y1 = sums_out(1)
    z_sum(1, 1)
    p2a.wait_recv()
    back(1 - xh, 0, (2,), True)
    z_sum(0, 3)
    y1n = sums_on(1, y1[0], y1[1])
    y2s = sums_out(2)
    z_sum(1, 2)
    end0 = z_last(0)
    y2n = sums_on(2, y2s[0], y2s[1])
    sums_in(0, (y0[2], y0[3], *y0n))
    z_sum(1, 3)
    sums_in(1, (y1[2], y1[3], *y1n))
    end1 = z_last(1)
    sums_in(2, (y2s[2], y2s[3], *y2n))
    arrived(end0)
    arrived(end1)
    for a in range(2):
        for b in range(2):
            total = (tr[a, b, 0].astype(F32) + tr[a, b, 1].astype(F32)).astype(BF16)
            for i in range(4):
                at = ((a * 4 + i) * 2 + b) * 256
                rows_out[:, at : at + 256] = total[:, i * 256 : (i + 1) * 256]
    gated = (a0, b0, s1, s2, g0, g1, g2b)
    for copy in sent:
        if not any(copy is one for one in gated):
            copy.wait_send()


def body(tokens, gate_weight, up_weight, cotangent):
    wides = [2 * wide for _, wide in CHUNKS]
    n = len(CHUNKS)
    dma = pltpu.SemaphoreType.DMA

    def per_chunk(*lead, dtype=BF16):
        return [pltpu.VMEM((*lead, wide), dtype) for wide in wides]

    vmem = pl.BlockSpec(memory_space=pltpu.VMEM)
    grid = pl.BlockSpec(memory_space=pl.ANY)
    tile = jax.ShapeDtypeStruct(gate_weight.shape, BF16)
    return pl.pallas_call(
        kernel,
        out_shape=(tile, jax.ShapeDtypeStruct(tokens.shape, BF16), tile, tile),
        in_specs=[vmem, grid, grid, vmem],
        out_specs=(vmem, vmem, vmem, vmem),
        scratch_shapes=[
            *per_chunk(4, 256),
            *per_chunk(2, 2, 128),
            *per_chunk(2, 2, 128),
            *per_chunk(2, 128),
            *per_chunk(2, 128),
            *per_chunk(2, 2, 128, dtype=F32),
            *per_chunk(2, 2, 2, 128),
            *per_chunk(4, 256),
            *per_chunk(2, 256),
            *per_chunk(2, 128),
            pltpu.VMEM((2, 2, 2, 2, 4, 16, 1024), BF16),
            pltpu.VMEM((1024, 1024), BF16),
            pltpu.VMEM((4, 16, 1024), BF16),
            pltpu.VMEM((2, 2, 2, 2, 4, 16, 1024), F32),
            pltpu.VMEM((2, 2, STEPS, 2, 2, 16, 1024), BF16),
            pltpu.VMEM((2, 2, STEPS, 2, 2, 16, 1024), BF16),
            pltpu.VMEM((2, 2, 2, 16, 1024), BF16),
            pltpu.VMEM((2, 2, 2, 16, 1024), BF16),
            dma((2 * n,)), dma((7,)), dma((7,)),
            dma((4, 4, 2)), dma((4, 4, 2)),
            dma((n, 4)), dma((n, 4)),
            dma((n, 9)), dma((n, 9)),
            dma((n, 6)), dma((n, 6)),
            dma((2, STEPS, 2, 2)), dma((2, STEPS, 2, 2)),
            dma((7,)), dma((7,)),
        ],
        compiler_params=pltpu.CompilerParams(
            collective_id=0, has_side_effects=True, vmem_limit_bytes=56 * 2**20
        ),
        name="swiglu",
    )(tokens, gate_weight, up_weight, cotangent)


def solution(mesh):
    torus = Mesh(mesh.devices.reshape(2, 4, 2, 2, 8), (*DP, *TENSOR))
    specs = (ROWS, BLOCK, BLOCK, BLOCK)
    outs = (BLOCK, ROWS, BLOCK, BLOCK)
    return jax.shard_map(body, mesh=torus, in_specs=specs, out_specs=outs, check_vma=False)
```

```python
import functools

import jax
import jax.numpy as jnp
from jax import lax
from jax.experimental import pallas as pl
from jax.experimental.pallas import tpu as pltpu
from jax.sharding import Mesh
from jax.sharding import PartitionSpec as P

SPLIT = ("xh", "c")
TENSOR = ("xl", "z")
DP = ("xh", "y", "c")
ROWS = P((*DP, *TENSOR), None)
BLOCK = P(DP, TENSOR)
MESH = pl.DeviceIdType.MESH
F32 = jnp.float32
BF16 = jnp.bfloat16
CHUNKS = ((0, 256), (256, 384), (640, 256))
NZ = 8
TILE = 256
OFFSETS = (0, 1, -1, 2, -2, 3, -3, 4)
CUBE = tuple((a, b, d) for a in range(2) for b in range(2) for d in range(2))
STEPS = 4


def dot(a, b):
    return jnp.dot(a, b, preferred_element_type=F32)


def dot_nt(a, b):
    return lax.dot_general(a, b, (((1,), (1,)), ((), ())), preferred_element_type=F32)


def kernel(tokens, gate, up, cot_far, hidden, rows_out, grad_gate, grad_up, *scratch):
    n = len(CHUNKS)
    W, PC, RC, PX, RX, PO, G, DW, RY, QY = (scratch[i * n : (i + 1) * n] for i in range(10))
    (
        x, xt, stage, cot_here, dx, zs, zr, ts, tr,
        loc, cs, cr, zgs, zgr, ws, wr, ms, mr, ys, yr, zrs, zrr, fs, fr,
    ) = scratch[10 * n :]
    xh, y, c, xl, z = (lax.axis_index(a) for a in ("xh", "y", "c", "xl", "z"))
    yp, ym, y2 = lax.rem(y + 1, 4), lax.rem(y + 3, 4), lax.rem(y + 2, 4)
    zp, zm = lax.rem(z + 1, NZ), lax.rem(z + NZ - 1, NZ)
    core, across = {"c": 1 - c}, {"xh": 1 - xh}
    sent = []

    def go(src, dst, send, recv, to):
        copy = pltpu.make_async_remote_copy(
            src_ref=src, dst_ref=dst, send_sem=send, recv_sem=recv,
            device_id=to, device_id_type=MESH,
        )
        copy.start()
        sent.append(copy)
        return copy

    def left(copy):
        copy.wait_send()
        sent[:] = [one for one in sent if one is not copy]

    def arrived(copies):
        for copy in copies:
            copy.wait_recv()

    def flip(a, b, d):
        return (1 - xh if a else xh, 1 - c if b else c, 1 - xl if d else xl)

    def cube_id(a, b, d):
        px, pc, plo = flip(a, b, d)
        return {"xh": px, "c": pc, "xl": plo}

    def slot(offset):
        return divmod(OFFSETS.index(offset if offset != -4 else 4), 4)

    def half(hs):
        return pl.ds(hs[0], len(hs))

    barrier = pltpu.get_barrier_semaphore()
    peers = [{"y": yp}, {"y": ym}, {"z": zp}, {"z": zm}] + [cube_id(*k) for k in CUBE[1:]]
    for peer in peers:
        pl.semaphore_signal(barrier, inc=1, device_id=peer, device_id_type=MESH)
    cot = cot_here
    cot_in = pltpu.make_async_copy(cot_far, cot, loc.at[2 * n])
    local = []
    for k, (at, wide) in enumerate(CHUNKS):
        for i, ref in enumerate((gate, up)):
            copy = pltpu.make_async_copy(
                ref.at[:, pl.ds(at, wide)], W[k].at[y, :, pl.ds(i * wide, wide)], loc.at[2 * k + i]
            )
            copy.start()
            local.append(copy)
    for a in range(2):
        for b in range(2):
            for i in range(4):
                at = ((a * 4 + i) * 2 + b) * 256
                stage[2 * a + b, :, i * 256 : (i + 1) * 256] = tokens[:, at : at + 256]
    x[0, c, xh, xl, 0] = stage[2 * xh + c]

    pl.semaphore_wait(barrier, len(peers))

    cube = [None]
    for k, key in enumerate(CUBE):
        if k:
            a, b, _ = flip(*key)
            cube.append(go(stage.at[2 * a + b], x.at[0, c, xh, xl, 0], cs.at[k - 1], cr.at[k - 1], cube_id(*key)))

    def send_weights(k):
        return (
            go(W[k].at[y], W[k].at[y], ws.at[k, 0], wr.at[k, 0], {"y": yp}),
            go(W[k].at[y], W[k].at[y], ws.at[k, 1], wr.at[k, 1], {"y": ym}),
        )

    def relay_weights(k):
        return (
            go(W[k].at[ym, pl.ds(0, 128)], W[k].at[ym, pl.ds(0, 128)], ws.at[k, 2], wr.at[k, 2], {"y": yp}),
            go(W[k].at[yp, pl.ds(128, 128)], W[k].at[yp, pl.ds(128, 128)], ws.at[k, 3], wr.at[k, 3], {"y": ym}),
        )

    for copy in local:
        copy.wait()
    cot_in.start()
    direct = [send_weights(0)]
    relay = []

    moving = {}

    def z_step(step):
        for i in range(4):
            if step == 0:
                arrived(cube[max(1, 2 * i) : 2 * i + 2])
            px, pc, _ = flip(i // 2, i % 2, 0)
            for way in range(2):
                if (step - 1, i, way) in moving:
                    moving[step - 1, i, way].wait_recv()
                if step == 3 and i // 2 != way:
                    continue
                sign = 1 if way else -1
                (h, at), (h2, to) = slot(sign * step), slot(sign * (step + 1))
                moving[step, i, way] = go(
                    x.at[h, pc, px, :, at], x.at[h2, pc, px, :, to],
                    zgs.at[step, i, way], zgr.at[step, i, way], {"z": zm if way else zp},
                )

    def columns(j):
        return pl.ds(pl.multiple_of(j * TILE, TILE), TILE)

    def matrix(ref, k):
        return ref[k][...].reshape(1024, 2 * CHUNKS[k][1])

    def forward(k, hs):
        sl, m, w = half(hs), len(hs), 2 * CHUNKS[k][1]
        value = dot(x[sl, 1 - c].reshape(256 * m, 1024), matrix(W, k))
        PC[k][sl] = value.astype(BF16).reshape(m, 2, 128, w)
        near = go(PC[k].at[sl], RC[k].at[sl], ms.at[k, hs[0]], mr.at[k, hs[0]], core)
        value = dot(x[sl, c].reshape(256 * m, 1024), matrix(W, k))
        PO[k][sl] = value.reshape(m, 2, 128, w)
        return near

    def join(k, hs, near):
        sl = half(hs)
        near.wait_recv()
        PX[k][sl] = (PO[k][sl, 1 - xh] + RC[k][sl, 1 - xh].astype(F32)).astype(BF16)

    def sums_across(k, hs):
        sl, i = half(hs), 2 + hs[0]
        return go(PX[k].at[sl], RX[k].at[sl], ms.at[k, i], mr.at[k, i], across)

    def grads_across(k, hs):
        part, i = G[k].at[half(hs), c, xh], 4 + hs[0]
        return go(part, part, ms.at[k, i], mr.at[k, i], across)

    def pass_on(k, hs):
        part, i = G[k].at[half(hs), c, 1 - xh], 7 + hs[0]
        return go(part, part, ms.at[k, i], mr.at[k, i], core)

    def middle(k):
        at, wide = CHUNKS[k]

        def step(i, _):
            h, j = i // 8, lax.rem(i, 8)
            rows = pl.ds(pl.multiple_of(j * 16, 16), 16)
            r = 4 * h + lax.rem(j, 4)
            there = lax.rem(z + NZ + (r + 1) // 2 * (2 * lax.rem(r, 2) - 1), NZ)
            place = pl.ds(pl.multiple_of((j // 4 * NZ + there) * 16, 16), 16)
            pre = PO[k][h, xh, rows, :] + RC[k][h, xh, rows, :].astype(F32) + RX[k][h, rows, :].astype(F32)
            gate_pre, up_pre = pre[:, :wide], pre[:, wide:]
            sigma = jax.nn.sigmoid(gate_pre)
            activation = gate_pre * sigma
            upstream = cot[place, pl.ds(at, wide)].astype(F32)
            slope = sigma * (1.0 + gate_pre * (1.0 - sigma))
            hidden[place, pl.ds(at, wide)] = (activation * up_pre).astype(BF16)
            G[k][h, c, xh, rows, pl.ds(0, wide)] = (upstream * up_pre * slope).astype(BF16)
            G[k][h, c, xh, rows, pl.ds(wide, wide)] = (upstream * activation).astype(BF16)
            return 0

        lax.fori_loop(0, 16, step, 0)
        part = G[k].at[:, c, xh]
        return go(part, part, ms.at[k, 6], mr.at[k, 6], core)

    def turn(i, _):
        at, j = i // 4, lax.rem(i, 4)
        cols = columns(j)
        xt[cols, columns(at)] = x[at // 2, lax.rem(at, 2), :, :, :, :, cols].reshape(256, TILE).T
        return 0

    def back(g, h, chunks, add):
        total = sum(
            dot_nt(G[k][h, :, g].reshape(256, 2 * CHUNKS[k][1]), matrix(W, k)) for k in chunks
        )
        total = total.reshape(2, 2, 4, 16, 1024)
        dx[h, :, g] = total + dx[h, :, g] if add else total

    flows = {}

    def z_sum(h, step):
        for b in range(2):
            gx, gc, _ = flip(h, b, 0)
            for way in range(2):
                if step == 0 and b != way:
                    continue
                far = STEPS - step
                side, at = slot(-far if way else far)
                value = dx[side, gc, gx, :, at]
                if (h, step - 1, way, b) in flows:
                    flows[h, step - 1, way, b].wait_recv()
                    value = value + zr[h, way, step - 1, b].astype(F32)
                zs[h, way, step, b] = value.astype(BF16)
                flows[h, step, way, b] = go(
                    zs.at[h, way, step, b], zr.at[h, way, step, b],
                    zrs.at[h, step, way, b], zrr.at[h, step, way, b], {"z": zm if way else zp},
                )

    def z_last(h):
        out = []
        for b in range(2):
            arrived((flows[h, 3, 0, b], flows[h, 3, 1, b]))
            gx, gc, _ = flip(h, b, 0)
            total = dx[0, gc, gx, :, 0] + zr[h, 0, 3, b].astype(F32) + zr[h, 1, 3, b].astype(F32)
            ts[gx, gc] = total.astype(BF16)
            for d in range(2):
                key = (h, b, d)
                k = CUBE.index(key)
                at = flip(*key)
                if k:
                    out.append(go(ts.at[at], tr.at[xh, c, xl], fs.at[k - 1], fr.at[k - 1], cube_id(*key)))
        if h == 0:
            tr[xh, c, xl] = ts[xh, c, xl]
        return out

    def weight_grad(k, at):
        DW[k][at] = dot(xt[columns(at), :], matrix(G, k)).astype(BF16)

    upper, lower = pl.ds(0, 128), pl.ds(128, 128)

    def sums_out(k):
        weight_grad(k, y2)
        a = go(DW[k].at[y2, upper], QY[k].at[0], ys.at[k, 0], yr.at[k, 0], {"y": yp})
        b = go(DW[k].at[y2, lower], QY[k].at[1], ys.at[k, 1], yr.at[k, 1], {"y": ym})
        weight_grad(k, yp)
        e = go(DW[k].at[yp, lower], RY[k].at[0, lower], ys.at[k, 2], yr.at[k, 2], {"y": yp})
        weight_grad(k, ym)
        f = go(DW[k].at[ym, upper], RY[k].at[1, upper], ys.at[k, 3], yr.at[k, 3], {"y": ym})
        return a, b, e, f

    def sums_on(k, a, b):
        a.wait_recv()
        DW[k][yp, upper] = (DW[k][yp, upper].astype(F32) + QY[k][0].astype(F32)).astype(BF16)
        e = go(DW[k].at[yp, upper], RY[k].at[0, upper], ys.at[k, 4], yr.at[k, 4], {"y": yp})
        b.wait_recv()
        DW[k][ym, lower] = (DW[k][ym, lower].astype(F32) + QY[k][1].astype(F32)).astype(BF16)
        f = go(DW[k].at[ym, lower], RY[k].at[1, lower], ys.at[k, 5], yr.at[k, 5], {"y": ym})
        return e, f

    def sums_in(k, copies):
        at, wide = CHUNKS[k]
        weight_grad(k, y)
        arrived(copies)

        def step(i, _):
            rows = pl.ds(pl.multiple_of(i * 32, 32), 32)
            total = DW[k][y, rows].astype(F32) + RY[k][0, rows].astype(F32) + RY[k][1, rows].astype(F32)
            total = total.astype(BF16)
            grad_gate[rows, pl.ds(at, wide)] = total[:, :wide]
            grad_up[rows, pl.ds(at, wide)] = total[:, wide:]
            return 0

        lax.fori_loop(0, 8, step, 0)

    z_step(0)
    for copy in direct[0]:
        left(copy)
    direct.append(send_weights(1))
    arrived(direct[0])
    relay.append(relay_weights(0))
    z_step(1)
    z_step(2)
    arrived(relay[0])
    near = forward(0, (0,))
    arrived(direct[1])
    relay.append(relay_weights(1))
    join(0, (0,), near)
    a0 = sums_across(0, (0,))
    z_step(3)
    for copy in relay[1]:
        left(copy)
    direct += [send_weights(k) for k in range(2, n)]
    arrived([moving[key] for key in moving if key[0] == 3])
    near = forward(0, (1,))
    arrived(relay[1])
    join(0, (1,), near)
    left(a0)
    b0 = sums_across(0, (1,))
    near = forward(1, (0, 1))
    lax.fori_loop(0, 16, turn, 0)
    join(1, (0, 1), near)
    left(b0)
    sums = [None, sums_across(1, (0, 1))]
    arrived((a0, b0))
    cot_in.wait()
    own = [middle(0)]
    for k in range(2, n):
        arrived(direct[k])
        relay.append(relay_weights(k))
    grads, passed, out, on = [], [], [], []
    for k in range(n - 2):
        left(sums[k + 1])
        grads.append(grads_across(k, (0, 1)))
        arrived(relay[k + 2])
        near = forward(k + 2, (0, 1))
        sums[k + 1].wait_recv()
        own.append(middle(k + 1))
        join(k + 2, (0, 1), near)
        left(grads[k])
        sums.append(sums_across(k + 2, (0, 1)))
        grads[k].wait_recv()
        passed.append(pass_on(k, (0, 1)))
        if k:
            on.append(sums_on(k - 1, *out[k - 1][:2]))
        arrived((own[k], passed[k]))
        out.append(sums_out(k))
    p, l = n - 2, n - 1
    most, every = tuple(range(n - 1)), tuple(range(n))
    left(sums[l])
    grads.append(grads_across(p, (0, 1)))
    sums[l].wait_recv()
    own.append(middle(l))
    on.append(sums_on(p - 1, *out[p - 1][:2]))
    arrived((own[p], own[l]))
    back(xh, 1, every, False)
    z_sum(0, 0)
    back(xh, 0, every, False)
    left(grads[p])
    far = grads_across(l, (1,))
    grads[p].wait_recv()
    passed.append(pass_on(p, (0, 1)))
    z_sum(0, 1)
    left(far)
    near = grads_across(l, (0,))
    passed[p].wait_recv()
    out.append(sums_out(p))
    far.wait_recv()
    far = pass_on(l, (1,))
    back(1 - xh, 1, most, False)
    far.wait_recv()
    back(1 - xh, 1, (l,), True)
    z_sum(1, 0)
    near.wait_recv()
    near = pass_on(l, (0,))
    back(1 - xh, 0, most, False)
    z_sum(0, 2)
    on.append(sums_on(p, *out[p][:2]))
    z_sum(1, 1)
    near.wait_recv()
    back(1 - xh, 0, (l,), True)
    out.append(sums_out(l))
    z_sum(1, 2)
    z_sum(0, 3)
    for k in range(p):
        sums_in(k, (*out[k][2:], *on[k]))
    z_sum(1, 3)
    on.append(sums_on(l, *out[l][:2]))
    end0 = z_last(0)
    sums_in(p, (*out[p][2:], *on[p]))
    end1 = z_last(1)
    sums_in(l, (*out[l][2:], *on[l]))
    arrived(end0)
    arrived(end1)
    for a in range(2):
        for b in range(2):
            total = (tr[a, b, 0].astype(F32) + tr[a, b, 1].astype(F32)).astype(BF16)
            for i in range(4):
                at = ((a * 4 + i) * 2 + b) * 256
                rows_out[:, at : at + 256] = total[:, i * 256 : (i + 1) * 256]
    for copy in sent:
        copy.wait_send()


def hand_over(*refs):
    n = len(refs) // 3
    here = refs[2 * n : 3 * n]
    into = [pltpu.make_async_copy(refs[i], here[i], refs[-1].at[i]) for i in range(n)]
    out = [pltpu.make_async_copy(here[i], refs[n + i], refs[-1].at[n + i]) for i in range(n)]
    for copy in into:
        copy.start()
    for i in range(n):
        into[i].wait()
        out[i].start()
    for copy in out:
        copy.wait()


def body(tokens, gate_weight, up_weight, cotangent):
    wides = [2 * wide for _, wide in CHUNKS]
    n = len(CHUNKS)
    dma = pltpu.SemaphoreType.DMA

    def per_chunk(*lead, dtype=BF16):
        return [pltpu.VMEM((*lead, wide), dtype) for wide in wides]

    vmem = pl.BlockSpec(memory_space=pltpu.VMEM)
    grid = pl.BlockSpec(memory_space=pl.ANY)
    tile = jax.ShapeDtypeStruct(gate_weight.shape, BF16)
    outs = pl.pallas_call(
        kernel,
        out_shape=(tile, jax.ShapeDtypeStruct(tokens.shape, BF16), tile, tile),
        in_specs=[vmem, grid, grid, grid],
        out_specs=(vmem, vmem, vmem, vmem),
        scratch_shapes=[
            *per_chunk(4, 256),
            *per_chunk(2, 2, 128),
            *per_chunk(2, 2, 128),
            *per_chunk(2, 128),
            *per_chunk(2, 128),
            *per_chunk(2, 2, 128, dtype=F32),
            *per_chunk(2, 2, 2, 128),
            *per_chunk(4, 256),
            *per_chunk(2, 256),
            *per_chunk(2, 128),
            pltpu.VMEM((2, 2, 2, 2, 4, 16, 1024), BF16),
            pltpu.VMEM((1024, 1024), BF16),
            pltpu.VMEM((4, 16, 1024), BF16),
            pltpu.VMEM(gate_weight.shape, BF16),
            pltpu.VMEM((2, 2, 2, 2, 4, 16, 1024), F32),
            pltpu.VMEM((2, 2, STEPS, 2, 2, 16, 1024), BF16),
            pltpu.VMEM((2, 2, STEPS, 2, 2, 16, 1024), BF16),
            pltpu.VMEM((2, 2, 2, 16, 1024), BF16),
            pltpu.VMEM((2, 2, 2, 16, 1024), BF16),
            dma((2 * n + 1,)), dma((7,)), dma((7,)),
            dma((4, 4, 2)), dma((4, 4, 2)),
            dma((n, 4)), dma((n, 4)),
            dma((n, 9)), dma((n, 9)),
            dma((n, 6)), dma((n, 6)),
            dma((2, STEPS, 2, 2)), dma((2, STEPS, 2, 2)),
            dma((7,)), dma((7,)),
        ],
        compiler_params=pltpu.CompilerParams(
            collective_id=0, has_side_effects=True, vmem_limit_bytes=56 * 2**20
        ),
        name="swiglu",
    )(tokens, gate_weight, up_weight, cotangent)
    return pl.pallas_call(
        hand_over,
        out_shape=tuple(jax.ShapeDtypeStruct(a.shape, a.dtype) for a in outs),
        in_specs=[grid] * len(outs),
        out_specs=(grid,) * len(outs),
        scratch_shapes=[*(pltpu.VMEM(a.shape, a.dtype) for a in outs), dma((2 * len(outs),))],
        name="hand_over",
    )(*outs)


def solution(mesh):
    torus = Mesh(mesh.devices.reshape(2, 4, 2, 2, 8), (*DP, *TENSOR))
    specs = (ROWS, BLOCK, BLOCK, BLOCK)
    outs = (BLOCK, ROWS, BLOCK, BLOCK)
    return jax.shard_map(body, mesh=torus, in_specs=specs, out_specs=outs, check_vma=False)
```

```python
import functools

import jax
import jax.numpy as jnp
from jax import lax
from jax.experimental import pallas as pl
from jax.experimental.pallas import tpu as pltpu
from jax.sharding import Mesh
from jax.sharding import PartitionSpec as P

SPLIT = ("xh", "c")
TENSOR = ("xl", "z")
DP = ("xh", "y", "c")
ROWS = P((*DP, *TENSOR), None)
BLOCK = P(DP, TENSOR)
MESH = pl.DeviceIdType.MESH
F32 = jnp.float32
BF16 = jnp.bfloat16
CHUNKS = ((0, 256), (256, 384), (640, 256))
NZ = 8
TILE = 256
OFFSETS = (0, 1, -1, 2, -2, 3, -3, 4)
CUBE = tuple((a, b, d) for a in range(2) for b in range(2) for d in range(2))
STEPS = 4


def dot(a, b):
    return jnp.dot(a, b, preferred_element_type=F32)


def dot_nt(a, b):
    return lax.dot_general(a, b, (((1,), (1,)), ((), ())), preferred_element_type=F32)


def kernel(tokens, gate, up, cot_far, hidden, rows_out, grad_gate, grad_up, *scratch):
    n = len(CHUNKS)
    W, PC, RC, PX, RX, PO, G, DW, RY, QY = (scratch[i * n : (i + 1) * n] for i in range(10))
    (
        x, xt, stage, cot_here, dx, zs, zr, ts, tr,
        loc, cs, cr, zgs, zgr, ws, wr, ms, mr, ys, yr, zrs, zrr, fs, fr,
    ) = scratch[10 * n :]
    xh, y, c, xl, z = (lax.axis_index(a) for a in ("xh", "y", "c", "xl", "z"))
    yp, ym, y2 = lax.rem(y + 1, 4), lax.rem(y + 3, 4), lax.rem(y + 2, 4)
    zp, zm = lax.rem(z + 1, NZ), lax.rem(z + NZ - 1, NZ)
    core, across = {"c": 1 - c}, {"xh": 1 - xh}
    sent = []

    def go(src, dst, send, recv, to):
        copy = pltpu.make_async_remote_copy(
            src_ref=src, dst_ref=dst, send_sem=send, recv_sem=recv,
            device_id=to, device_id_type=MESH,
        )
        copy.start()
        sent.append(copy)
        return copy

    def left(copy):
        copy.wait_send()
        sent[:] = [one for one in sent if one is not copy]

    def arrived(copies):
        for copy in copies:
            copy.wait_recv()

    def flip(a, b, d):
        return (1 - xh if a else xh, 1 - c if b else c, 1 - xl if d else xl)

    def cube_id(a, b, d):
        px, pc, plo = flip(a, b, d)
        return {"xh": px, "c": pc, "xl": plo}

    def slot(offset):
        return divmod(OFFSETS.index(offset if offset != -4 else 4), 4)

    def half(hs):
        return pl.ds(hs[0], len(hs))

    barrier = pltpu.get_barrier_semaphore()
    peers = [{"y": yp}, {"y": ym}, {"y": y2}, {"z": zp}, {"z": zm}] + [cube_id(*k) for k in CUBE[1:]]
    for peer in peers:
        pl.semaphore_signal(barrier, inc=1, device_id=peer, device_id_type=MESH)
    cot = cot_here
    cot_in = pltpu.make_async_copy(cot_far, cot, loc.at[2 * n])
    local = []
    for k, (at, wide) in enumerate(CHUNKS):
        for i, ref in enumerate((gate, up)):
            copy = pltpu.make_async_copy(
                ref.at[:, pl.ds(at, wide)], W[k].at[y, :, pl.ds(i * wide, wide)], loc.at[2 * k + i]
            )
            copy.start()
            local.append(copy)
    for a in range(2):
        for b in range(2):
            for i in range(4):
                at = ((a * 4 + i) * 2 + b) * 256
                stage[2 * a + b, :, i * 256 : (i + 1) * 256] = tokens[:, at : at + 256]
    x[0, c, xh, xl, 0] = stage[2 * xh + c]

    pl.semaphore_wait(barrier, len(peers))

    cube = [None]
    for k, key in enumerate(CUBE):
        if k:
            a, b, _ = flip(*key)
            cube.append(go(stage.at[2 * a + b], x.at[0, c, xh, xl, 0], cs.at[k - 1], cr.at[k - 1], cube_id(*key)))

    def send_weights(k):
        return (
            go(W[k].at[y], W[k].at[y], ws.at[k, 0], wr.at[k, 0], {"y": yp}),
            go(W[k].at[y], W[k].at[y], ws.at[k, 1], wr.at[k, 1], {"y": ym}),
        )

    def relay_weights(k):
        return (
            go(W[k].at[ym, pl.ds(0, 128)], W[k].at[ym, pl.ds(0, 128)], ws.at[k, 2], wr.at[k, 2], {"y": yp}),
            go(W[k].at[yp, pl.ds(128, 128)], W[k].at[yp, pl.ds(128, 128)], ws.at[k, 3], wr.at[k, 3], {"y": ym}),
        )

    for copy in local:
        copy.wait()
    cot_in.start()
    direct = [send_weights(0)]
    relay = []

    moving = {}

    def z_step(step):
        for i in range(4):
            if step == 0:
                arrived(cube[max(1, 2 * i) : 2 * i + 2])
            px, pc, _ = flip(i // 2, i % 2, 0)
            for way in range(2):
                if (step - 1, i, way) in moving:
                    moving[step - 1, i, way].wait_recv()
                if step == 3 and i // 2 != way:
                    continue
                sign = 1 if way else -1
                (h, at), (h2, to) = slot(sign * step), slot(sign * (step + 1))
                moving[step, i, way] = go(
                    x.at[h, pc, px, :, at], x.at[h2, pc, px, :, to],
                    zgs.at[step, i, way], zgr.at[step, i, way], {"z": zm if way else zp},
                )

    def columns(j):
        return pl.ds(pl.multiple_of(j * TILE, TILE), TILE)

    def matrix(ref, k):
        return ref[k][...].reshape(1024, 2 * CHUNKS[k][1])

    def forward(k, hs):
        sl, m, w = half(hs), len(hs), 2 * CHUNKS[k][1]
        value = dot(x[sl, 1 - c].reshape(256 * m, 1024), matrix(W, k))
        PC[k][sl] = value.astype(BF16).reshape(m, 2, 128, w)
        near = go(PC[k].at[sl], RC[k].at[sl], ms.at[k, hs[0]], mr.at[k, hs[0]], core)
        value = dot(x[sl, c].reshape(256 * m, 1024), matrix(W, k))
        PO[k][sl] = value.reshape(m, 2, 128, w)
        return near

    def join(k, hs, near):
        sl = half(hs)
        near.wait_recv()
        PX[k][sl] = (PO[k][sl, 1 - xh] + RC[k][sl, 1 - xh].astype(F32)).astype(BF16)

    def sums_across(k, hs):
        sl, i = half(hs), 2 + hs[0]
        return go(PX[k].at[sl], RX[k].at[sl], ms.at[k, i], mr.at[k, i], across)

    def grads_across(k, hs):
        part, i = G[k].at[half(hs), c, xh], 4 + hs[0]
        return go(part, part, ms.at[k, i], mr.at[k, i], across)

    def pass_on(k, hs):
        part, i = G[k].at[half(hs), c, 1 - xh], 7 + hs[0]
        return go(part, part, ms.at[k, i], mr.at[k, i], core)

    def middle(k):
        at, wide = CHUNKS[k]

        def step(i, _):
            h, j = i // 8, lax.rem(i, 8)
            rows = pl.ds(pl.multiple_of(j * 16, 16), 16)
            r = 4 * h + lax.rem(j, 4)
            there = lax.rem(z + NZ + (r + 1) // 2 * (2 * lax.rem(r, 2) - 1), NZ)
            place = pl.ds(pl.multiple_of((j // 4 * NZ + there) * 16, 16), 16)
            pre = PO[k][h, xh, rows, :] + RC[k][h, xh, rows, :].astype(F32) + RX[k][h, rows, :].astype(F32)
            gate_pre, up_pre = pre[:, :wide], pre[:, wide:]
            sigma = jax.nn.sigmoid(gate_pre)
            activation = gate_pre * sigma
            upstream = cot[place, pl.ds(at, wide)].astype(F32)
            slope = sigma * (1.0 + gate_pre * (1.0 - sigma))
            hidden[place, pl.ds(at, wide)] = (activation * up_pre).astype(BF16)
            G[k][h, c, xh, rows, pl.ds(0, wide)] = (upstream * up_pre * slope).astype(BF16)
            G[k][h, c, xh, rows, pl.ds(wide, wide)] = (upstream * activation).astype(BF16)
            return 0

        lax.fori_loop(0, 16, step, 0)
        part = G[k].at[:, c, xh]
        return go(part, part, ms.at[k, 6], mr.at[k, 6], core)

    def turn(i, _):
        at, j = i // 4, lax.rem(i, 4)
        cols = columns(j)
        xt[cols, columns(at)] = x[at // 2, lax.rem(at, 2), :, :, :, :, cols].reshape(256, TILE).T
        return 0

    def back(g, h, chunks, add):
        total = sum(
            dot_nt(G[k][h, :, g].reshape(256, 2 * CHUNKS[k][1]), matrix(W, k)) for k in chunks
        )
        total = total.reshape(2, 2, 4, 16, 1024)
        dx[h, :, g] = total + dx[h, :, g] if add else total

    flows = {}

    def z_sum(h, step):
        for b in range(2):
            gx, gc, _ = flip(h, b, 0)
            for way in range(2):
                if step == 0 and b != way:
                    continue
                far = STEPS - step
                side, at = slot(-far if way else far)
                value = dx[side, gc, gx, :, at]
                if (h, step - 1, way, b) in flows:
                    flows[h, step - 1, way, b].wait_recv()
                    value = value + zr[h, way, step - 1, b].astype(F32)
                zs[h, way, step, b] = value.astype(BF16)
                flows[h, step, way, b] = go(
                    zs.at[h, way, step, b], zr.at[h, way, step, b],
                    zrs.at[h, step, way, b], zrr.at[h, step, way, b], {"z": zm if way else zp},
                )

    def z_last(h):
        out = []
        for b in range(2):
            arrived((flows[h, 3, 0, b], flows[h, 3, 1, b]))
            gx, gc, _ = flip(h, b, 0)
            total = dx[0, gc, gx, :, 0] + zr[h, 0, 3, b].astype(F32) + zr[h, 1, 3, b].astype(F32)
            ts[gx, gc] = total.astype(BF16)
            for d in range(2):
                key = (h, b, d)
                k = CUBE.index(key)
                at = flip(*key)
                if k:
                    out.append(go(ts.at[at], tr.at[xh, c, xl], fs.at[k - 1], fr.at[k - 1], cube_id(*key)))
        if h == 0:
            tr[xh, c, xl] = ts[xh, c, xl]
        return out

    def weight_grad(k, at):
        DW[k][at] = dot(xt[columns(at), :], matrix(G, k)).astype(BF16)

    upper, lower = pl.ds(0, 128), pl.ds(128, 128)

    def sums_out(k):
        weight_grad(k, y2)
        a = go(DW[k].at[y2, upper], QY[k].at[0], ys.at[k, 0], yr.at[k, 0], {"y": yp})
        b = go(DW[k].at[y2, lower], QY[k].at[1], ys.at[k, 1], yr.at[k, 1], {"y": ym})
        weight_grad(k, yp)
        e = go(DW[k].at[yp, lower], RY[k].at[0, lower], ys.at[k, 2], yr.at[k, 2], {"y": yp})
        weight_grad(k, ym)
        f = go(DW[k].at[ym, upper], RY[k].at[1, upper], ys.at[k, 3], yr.at[k, 3], {"y": ym})
        return a, b, e, f

    def sums_direct(k):
        weight_grad(k, y2)
        a = go(DW[k].at[y2, upper], QY[k].at[0], ys.at[k, 0], yr.at[k, 0], {"y": y2})
        b = go(DW[k].at[y2, lower], QY[k].at[1], ys.at[k, 1], yr.at[k, 1], {"y": y2})
        weight_grad(k, yp)
        e = go(DW[k].at[yp], RY[k].at[0], ys.at[k, 2], yr.at[k, 2], {"y": yp})
        weight_grad(k, ym)
        f = go(DW[k].at[ym], RY[k].at[1], ys.at[k, 3], yr.at[k, 3], {"y": ym})
        return a, b, e, f

    def sums_on(k, a, b):
        a.wait_recv()
        DW[k][yp, upper] = (DW[k][yp, upper].astype(F32) + QY[k][0].astype(F32)).astype(BF16)
        e = go(DW[k].at[yp, upper], RY[k].at[0, upper], ys.at[k, 4], yr.at[k, 4], {"y": yp})
        b.wait_recv()
        DW[k][ym, lower] = (DW[k][ym, lower].astype(F32) + QY[k][1].astype(F32)).astype(BF16)
        f = go(DW[k].at[ym, lower], RY[k].at[1, lower], ys.at[k, 5], yr.at[k, 5], {"y": ym})
        return e, f

    def sums_in(k, copies, direct=False):
        at, wide = CHUNKS[k]
        weight_grad(k, y)
        arrived(copies)

        def step(i, _):
            rows = pl.ds(pl.multiple_of(i * 32, 32), 32)
            total = DW[k][y, rows].astype(F32) + RY[k][0, rows].astype(F32) + RY[k][1, rows].astype(F32)
            if direct:
                there = pl.ds(pl.multiple_of(lax.rem(i, 4) * 32, 32), 32)
                total = total + QY[k][i // 4, there].astype(F32)
            total = total.astype(BF16)
            grad_gate[rows, pl.ds(at, wide)] = total[:, :wide]
            grad_up[rows, pl.ds(at, wide)] = total[:, wide:]
            return 0

        lax.fori_loop(0, 8, step, 0)

    z_step(0)
    for copy in direct[0]:
        left(copy)
    direct.append(send_weights(1))
    arrived(direct[0])
    relay.append(relay_weights(0))
    z_step(1)
    z_step(2)
    arrived(relay[0])
    near = forward(0, (0,))
    arrived(direct[1])
    relay.append(relay_weights(1))
    join(0, (0,), near)
    a0 = sums_across(0, (0,))
    z_step(3)
    for copy in relay[1]:
        left(copy)
    direct += [send_weights(k) for k in range(2, n)]
    arrived([moving[key] for key in moving if key[0] == 3])
    near = forward(0, (1,))
    arrived(relay[1])
    join(0, (1,), near)
    left(a0)
    b0 = sums_across(0, (1,))
    near = forward(1, (0, 1))
    lax.fori_loop(0, 16, turn, 0)
    join(1, (0, 1), near)
    left(b0)
    sums = [None, sums_across(1, (0, 1))]
    arrived((a0, b0))
    cot_in.wait()
    own = [middle(0)]
    for k in range(2, n):
        arrived(direct[k])
        relay.append(relay_weights(k))
    grads, passed, out, on = [], [], [], []
    for k in range(n - 2):
        left(sums[k + 1])
        grads.append(grads_across(k, (0, 1)))
        arrived(relay[k + 2])
        near = forward(k + 2, (0, 1))
        sums[k + 1].wait_recv()
        own.append(middle(k + 1))
        join(k + 2, (0, 1), near)
        left(grads[k])
        sums.append(sums_across(k + 2, (0, 1)))
        grads[k].wait_recv()
        passed.append(pass_on(k, (0, 1)))
        if k:
            on.append(sums_on(k - 1, *out[k - 1][:2]))
        arrived((own[k], passed[k]))
        out.append(sums_out(k))
    p, l = n - 2, n - 1
    most, every = tuple(range(n - 1)), tuple(range(n))
    left(sums[l])
    grads.append(grads_across(p, (0, 1)))
    sums[l].wait_recv()
    own.append(middle(l))
    on.append(sums_on(p - 1, *out[p - 1][:2]))
    arrived((own[p], own[l]))
    back(xh, 1, every, False)
    z_sum(0, 0)
    back(xh, 0, every, False)
    left(grads[p])
    far = grads_across(l, (1,))
    grads[p].wait_recv()
    passed.append(pass_on(p, (0, 1)))
    z_sum(0, 1)
    left(far)
    near = grads_across(l, (0,))
    passed[p].wait_recv()
    out.append(sums_out(p))
    z_sum(0, 2)
    far.wait_recv()
    far = pass_on(l, (1,))
    back(1 - xh, 1, most, False)
    far.wait_recv()
    back(1 - xh, 1, (l,), True)
    z_sum(1, 0)
    near.wait_recv()
    near = pass_on(l, (0,))
    back(1 - xh, 0, most, False)
    on.append(sums_on(p, *out[p][:2]))
    z_sum(1, 1)
    z_sum(0, 3)
    near.wait_recv()
    back(1 - xh, 0, (l,), True)
    out.append(sums_direct(l))
    z_sum(1, 2)
    for k in range(p):
        sums_in(k, (*out[k][2:], *on[k]))
    z_sum(1, 3)
    end0 = z_last(0)
    sums_in(p, (*out[p][2:], *on[p]))
    end1 = z_last(1)
    sums_in(l, out[l], True)
    arrived(end0)
    arrived(end1)
    for a in range(2):
        for b in range(2):
            total = (tr[a, b, 0].astype(F32) + tr[a, b, 1].astype(F32)).astype(BF16)
            for i in range(4):
                at = ((a * 4 + i) * 2 + b) * 256
                rows_out[:, at : at + 256] = total[:, i * 256 : (i + 1) * 256]
    for copy in sent:
        copy.wait_send()


def hand_over(*refs):
    n = len(refs) // 3
    here = refs[2 * n : 3 * n]
    into = [pltpu.make_async_copy(refs[i], here[i], refs[-1].at[i]) for i in range(n)]
    out = [pltpu.make_async_copy(here[i], refs[n + i], refs[-1].at[n + i]) for i in range(n)]
    for copy in into:
        copy.start()
    for i in range(n):
        into[i].wait()
        out[i].start()
    for copy in out:
        copy.wait()


def body(tokens, gate_weight, up_weight, cotangent):
    wides = [2 * wide for _, wide in CHUNKS]
    n = len(CHUNKS)
    dma = pltpu.SemaphoreType.DMA

    def per_chunk(*lead, dtype=BF16):
        return [pltpu.VMEM((*lead, wide), dtype) for wide in wides]

    vmem = pl.BlockSpec(memory_space=pltpu.VMEM)
    grid = pl.BlockSpec(memory_space=pl.ANY)
    tile = jax.ShapeDtypeStruct(gate_weight.shape, BF16)
    outs = pl.pallas_call(
        kernel,
        out_shape=(tile, jax.ShapeDtypeStruct(tokens.shape, BF16), tile, tile),
        in_specs=[vmem, grid, grid, grid],
        out_specs=(vmem, vmem, vmem, vmem),
        scratch_shapes=[
            *per_chunk(4, 256),
            *per_chunk(2, 2, 128),
            *per_chunk(2, 2, 128),
            *per_chunk(2, 128),
            *per_chunk(2, 128),
            *per_chunk(2, 2, 128, dtype=F32),
            *per_chunk(2, 2, 2, 128),
            *per_chunk(4, 256),
            *per_chunk(2, 256),
            *per_chunk(2, 128),
            pltpu.VMEM((2, 2, 2, 2, 4, 16, 1024), BF16),
            pltpu.VMEM((1024, 1024), BF16),
            pltpu.VMEM((4, 16, 1024), BF16),
            pltpu.VMEM(gate_weight.shape, BF16),
            pltpu.VMEM((2, 2, 2, 2, 4, 16, 1024), F32),
            pltpu.VMEM((2, 2, STEPS, 2, 2, 16, 1024), BF16),
            pltpu.VMEM((2, 2, STEPS, 2, 2, 16, 1024), BF16),
            pltpu.VMEM((2, 2, 2, 16, 1024), BF16),
            pltpu.VMEM((2, 2, 2, 16, 1024), BF16),
            dma((2 * n + 1,)), dma((7,)), dma((7,)),
            dma((4, 4, 2)), dma((4, 4, 2)),
            dma((n, 4)), dma((n, 4)),
            dma((n, 9)), dma((n, 9)),
            dma((n, 6)), dma((n, 6)),
            dma((2, STEPS, 2, 2)), dma((2, STEPS, 2, 2)),
            dma((7,)), dma((7,)),
        ],
        compiler_params=pltpu.CompilerParams(
            collective_id=0, has_side_effects=True, vmem_limit_bytes=56 * 2**20
        ),
        name="swiglu",
    )(tokens, gate_weight, up_weight, cotangent)
    return pl.pallas_call(
        hand_over,
        out_shape=tuple(jax.ShapeDtypeStruct(a.shape, a.dtype) for a in outs),
        in_specs=[grid] * len(outs),
        out_specs=(grid,) * len(outs),
        scratch_shapes=[*(pltpu.VMEM(a.shape, a.dtype) for a in outs), dma((2 * len(outs),))],
        name="hand_over",
    )(*outs)


def solution(mesh):
    torus = Mesh(mesh.devices.reshape(2, 4, 2, 2, 8), (*DP, *TENSOR))
    specs = (ROWS, BLOCK, BLOCK, BLOCK)
    outs = (BLOCK, ROWS, BLOCK, BLOCK)
    return jax.shard_map(body, mesh=torus, in_specs=specs, out_specs=outs, check_vma=False)
```

```python
import functools

import jax
import jax.numpy as jnp
from jax import lax
from jax.experimental import pallas as pl
from jax.experimental.pallas import tpu as pltpu
from jax.sharding import Mesh
from jax.sharding import PartitionSpec as P

SPLIT = ("xh", "c")
TENSOR = ("xl", "z")
DP = ("xh", "y", "c")
ROWS = P((*DP, *TENSOR), None)
BLOCK = P(DP, TENSOR)
MESH = pl.DeviceIdType.MESH
F32 = jnp.float32
BF16 = jnp.bfloat16
CHUNKS = ((0, 256), (256, 384), (640, 256))
NZ = 8
TILE = 256
OFFSETS = (0, 1, -1, 2, -2, 3, -3, 4)
CUBE = tuple((a, b, d) for a in range(2) for b in range(2) for d in range(2))
STEPS = 4


def dot(a, b):
    return jnp.dot(a, b, preferred_element_type=F32)


def dot_nt(a, b):
    return lax.dot_general(a, b, (((1,), (1,)), ((), ())), preferred_element_type=F32)


def kernel(tokens, gate, up, cot_far, hidden, rows_out, grad_gate, grad_up, *scratch):
    n = len(CHUNKS)
    W, PC, RC, PX, RX, PO, G, DW, RY, QY = (scratch[i * n : (i + 1) * n] for i in range(10))
    (
        x, xt, stage, cot_here, dx, zs, zr, ts, tr,
        loc, cs, cr, zgs, zgr, ws, wr, ms, mr, ys, yr, zrs, zrr, fs, fr,
    ) = scratch[10 * n :]
    xh, y, c, xl, z = (lax.axis_index(a) for a in ("xh", "y", "c", "xl", "z"))
    yp, ym, y2 = lax.rem(y + 1, 4), lax.rem(y + 3, 4), lax.rem(y + 2, 4)
    zp, zm = lax.rem(z + 1, NZ), lax.rem(z + NZ - 1, NZ)
    core, across = {"c": 1 - c}, {"xh": 1 - xh}
    sent = []

    def go(src, dst, send, recv, to):
        copy = pltpu.make_async_remote_copy(
            src_ref=src, dst_ref=dst, send_sem=send, recv_sem=recv,
            device_id=to, device_id_type=MESH,
        )
        copy.start()
        sent.append(copy)
        return copy

    def left(copy):
        copy.wait_send()
        sent[:] = [one for one in sent if one is not copy]

    def arrived(copies):
        for copy in copies:
            copy.wait_recv()

    def flip(a, b, d):
        return (1 - xh if a else xh, 1 - c if b else c, 1 - xl if d else xl)

    def cube_id(a, b, d):
        px, pc, plo = flip(a, b, d)
        return {"xh": px, "c": pc, "xl": plo}

    def slot(offset):
        return divmod(OFFSETS.index(offset if offset != -4 else 4), 4)

    def half(hs):
        return pl.ds(hs[0], len(hs))

    barrier = pltpu.get_barrier_semaphore()
    peers = [{"y": yp}, {"y": ym}, {"y": y2}, {"z": zp}, {"z": zm}] + [cube_id(*k) for k in CUBE[1:]]
    for peer in peers:
        pl.semaphore_signal(barrier, inc=1, device_id=peer, device_id_type=MESH)
    cot = cot_here
    cot_in = pltpu.make_async_copy(cot_far, cot, loc.at[2 * n])
    local = []
    for k, (at, wide) in enumerate(CHUNKS):
        for i, ref in enumerate((gate, up)):
            copy = pltpu.make_async_copy(
                ref.at[:, pl.ds(at, wide)], W[k].at[y, :, pl.ds(i * wide, wide)], loc.at[2 * k + i]
            )
            copy.start()
            local.append(copy)
    for a in range(2):
        for b in range(2):
            for i in range(4):
                at = ((a * 4 + i) * 2 + b) * 256
                stage[2 * a + b, :, i * 256 : (i + 1) * 256] = tokens[:, at : at + 256]
    x[0, c, xh, xl, 0] = stage[2 * xh + c]

    pl.semaphore_wait(barrier, len(peers))

    cube = [None]
    for k, key in enumerate(CUBE):
        if k:
            a, b, _ = flip(*key)
            cube.append(go(stage.at[2 * a + b], x.at[0, c, xh, xl, 0], cs.at[k - 1], cr.at[k - 1], cube_id(*key)))

    def send_weights(k):
        return (
            go(W[k].at[y], W[k].at[y], ws.at[k, 0], wr.at[k, 0], {"y": yp}),
            go(W[k].at[y], W[k].at[y], ws.at[k, 1], wr.at[k, 1], {"y": ym}),
        )

    def relay_weights(k):
        return (
            go(W[k].at[ym, pl.ds(0, 128)], W[k].at[ym, pl.ds(0, 128)], ws.at[k, 2], wr.at[k, 2], {"y": yp}),
            go(W[k].at[yp, pl.ds(128, 128)], W[k].at[yp, pl.ds(128, 128)], ws.at[k, 3], wr.at[k, 3], {"y": ym}),
        )

    for copy in local:
        copy.wait()
    cot_in.start()
    direct = [send_weights(0)]
    relay = []

    moving = {}

    def z_step(step):
        for i in range(4):
            if step == 0:
                arrived(cube[max(1, 2 * i) : 2 * i + 2])
            px, pc, _ = flip(i // 2, i % 2, 0)
            for way in range(2):
                if (step - 1, i, way) in moving:
                    moving[step - 1, i, way].wait_recv()
                if step == 3 and i // 2 != way:
                    continue
                sign = 1 if way else -1
                (h, at), (h2, to) = slot(sign * step), slot(sign * (step + 1))
                moving[step, i, way] = go(
                    x.at[h, pc, px, :, at], x.at[h2, pc, px, :, to],
                    zgs.at[step, i, way], zgr.at[step, i, way], {"z": zm if way else zp},
                )

    def columns(j):
        return pl.ds(pl.multiple_of(j * TILE, TILE), TILE)

    def matrix(ref, k):
        return ref[k][...].reshape(1024, 2 * CHUNKS[k][1])

    def forward(k, hs):
        sl, m, w = half(hs), len(hs), 2 * CHUNKS[k][1]
        value = dot(x[sl, 1 - c].reshape(256 * m, 1024), matrix(W, k))
        PC[k][sl] = value.astype(BF16).reshape(m, 2, 128, w)
        near = go(PC[k].at[sl], RC[k].at[sl], ms.at[k, hs[0]], mr.at[k, hs[0]], core)
        value = dot(x[sl, c].reshape(256 * m, 1024), matrix(W, k))
        PO[k][sl] = value.reshape(m, 2, 128, w)
        return near

    def join(k, hs, near):
        sl = half(hs)
        near.wait_recv()
        PX[k][sl] = (PO[k][sl, 1 - xh] + RC[k][sl, 1 - xh].astype(F32)).astype(BF16)

    def sums_across(k, hs):
        sl, i = half(hs), 2 + hs[0]
        return go(PX[k].at[sl], RX[k].at[sl], ms.at[k, i], mr.at[k, i], across)

    def grads_across(k, hs):
        part, i = G[k].at[half(hs), c, xh], 4 + hs[0]
        return go(part, part, ms.at[k, i], mr.at[k, i], across)

    def pass_on(k, hs):
        part, i = G[k].at[half(hs), c, 1 - xh], 7 + hs[0]
        return go(part, part, ms.at[k, i], mr.at[k, i], core)

    def middle(k):
        at, wide = CHUNKS[k]

        def step(i, _):
            h, j = i // 8, lax.rem(i, 8)
            rows = pl.ds(pl.multiple_of(j * 16, 16), 16)
            r = 4 * h + lax.rem(j, 4)
            there = lax.rem(z + NZ + (r + 1) // 2 * (2 * lax.rem(r, 2) - 1), NZ)
            place = pl.ds(pl.multiple_of((j // 4 * NZ + there) * 16, 16), 16)
            pre = PO[k][h, xh, rows, :] + RC[k][h, xh, rows, :].astype(F32) + RX[k][h, rows, :].astype(F32)
            gate_pre, up_pre = pre[:, :wide], pre[:, wide:]
            sigma = jax.nn.sigmoid(gate_pre)
            activation = gate_pre * sigma
            upstream = cot[place, pl.ds(at, wide)].astype(F32)
            slope = sigma * (1.0 + gate_pre * (1.0 - sigma))
            hidden[place, pl.ds(at, wide)] = (activation * up_pre).astype(BF16)
            G[k][h, c, xh, rows, pl.ds(0, wide)] = (upstream * up_pre * slope).astype(BF16)
            G[k][h, c, xh, rows, pl.ds(wide, wide)] = (upstream * activation).astype(BF16)
            return 0

        lax.fori_loop(0, 16, step, 0)
        part = G[k].at[:, c, xh]
        return go(part, part, ms.at[k, 6], mr.at[k, 6], core)

    def turn(i, _):
        at, j = i // 4, lax.rem(i, 4)
        cols = columns(j)
        xt[cols, columns(at)] = x[at // 2, lax.rem(at, 2), :, :, :, :, cols].reshape(256, TILE).T
        return 0

    def back(g, h, chunks, add):
        total = sum(
            dot_nt(G[k][h, :, g].reshape(256, 2 * CHUNKS[k][1]), matrix(W, k)) for k in chunks
        )
        total = total.reshape(2, 2, 4, 16, 1024)
        dx[h, :, g] = total + dx[h, :, g] if add else total

    flows = {}

    def z_sum(h, step):
        for b in range(2):
            gx, gc, _ = flip(h, b, 0)
            for way in range(2):
                if step == 0 and b != way:
                    continue
                far = STEPS - step
                side, at = slot(-far if way else far)
                value = dx[side, gc, gx, :, at]
                if (h, step - 1, way, b) in flows:
                    flows[h, step - 1, way, b].wait_recv()
                    value = value + zr[h, way, step - 1, b].astype(F32)
                zs[h, way, step, b] = value.astype(BF16)
                flows[h, step, way, b] = go(
                    zs.at[h, way, step, b], zr.at[h, way, step, b],
                    zrs.at[h, step, way, b], zrr.at[h, step, way, b], {"z": zm if way else zp},
                )

    def z_last(h):
        out = []
        for b in range(2):
            arrived((flows[h, 3, 0, b], flows[h, 3, 1, b]))
            gx, gc, _ = flip(h, b, 0)
            total = dx[0, gc, gx, :, 0] + zr[h, 0, 3, b].astype(F32) + zr[h, 1, 3, b].astype(F32)
            ts[gx, gc] = total.astype(BF16)
            for d in range(2):
                key = (h, b, d)
                k = CUBE.index(key)
                at = flip(*key)
                if k:
                    out.append(go(ts.at[at], tr.at[xh, c, xl], fs.at[k - 1], fr.at[k - 1], cube_id(*key)))
        if h == 0:
            tr[xh, c, xl] = ts[xh, c, xl]
        return out

    def weight_grad(k, at):
        DW[k][at] = dot(xt[columns(at), :], matrix(G, k)).astype(BF16)

    upper, lower = pl.ds(0, 128), pl.ds(128, 128)

    def sums_out(k):
        weight_grad(k, y2)
        a = go(DW[k].at[y2, upper], QY[k].at[0], ys.at[k, 0], yr.at[k, 0], {"y": yp})
        b = go(DW[k].at[y2, lower], QY[k].at[1], ys.at[k, 1], yr.at[k, 1], {"y": ym})
        weight_grad(k, yp)
        e = go(DW[k].at[yp, lower], RY[k].at[0, lower], ys.at[k, 2], yr.at[k, 2], {"y": yp})
        weight_grad(k, ym)
        f = go(DW[k].at[ym, upper], RY[k].at[1, upper], ys.at[k, 3], yr.at[k, 3], {"y": ym})
        return a, b, e, f

    def sums_direct(k):
        weight_grad(k, y2)
        a = go(DW[k].at[y2, upper], QY[k].at[0], ys.at[k, 0], yr.at[k, 0], {"y": y2})
        b = go(DW[k].at[y2, lower], QY[k].at[1], ys.at[k, 1], yr.at[k, 1], {"y": y2})
        weight_grad(k, yp)
        e = go(DW[k].at[yp], RY[k].at[0], ys.at[k, 2], yr.at[k, 2], {"y": yp})
        weight_grad(k, ym)
        f = go(DW[k].at[ym], RY[k].at[1], ys.at[k, 3], yr.at[k, 3], {"y": ym})
        return a, b, e, f

    def sums_on(k, a, b):
        a.wait_recv()
        DW[k][yp, upper] = (DW[k][yp, upper].astype(F32) + QY[k][0].astype(F32)).astype(BF16)
        e = go(DW[k].at[yp, upper], RY[k].at[0, upper], ys.at[k, 4], yr.at[k, 4], {"y": yp})
        b.wait_recv()
        DW[k][ym, lower] = (DW[k][ym, lower].astype(F32) + QY[k][1].astype(F32)).astype(BF16)
        f = go(DW[k].at[ym, lower], RY[k].at[1, lower], ys.at[k, 5], yr.at[k, 5], {"y": ym})
        return e, f

    def sums_in(k, copies, direct=False):
        at, wide = CHUNKS[k]
        weight_grad(k, y)
        arrived(copies)

        def step(i, _):
            rows = pl.ds(pl.multiple_of(i * 32, 32), 32)
            total = DW[k][y, rows].astype(F32) + RY[k][0, rows].astype(F32) + RY[k][1, rows].astype(F32)
            if direct:
                there = pl.ds(pl.multiple_of(lax.rem(i, 4) * 32, 32), 32)
                total = total + QY[k][i // 4, there].astype(F32)
            total = total.astype(BF16)
            grad_gate[rows, pl.ds(at, wide)] = total[:, :wide]
            grad_up[rows, pl.ds(at, wide)] = total[:, wide:]
            return 0

        lax.fori_loop(0, 8, step, 0)

    z_step(0)
    for copy in direct[0]:
        left(copy)
    direct.append(send_weights(1))
    arrived(direct[0])
    relay.append(relay_weights(0))
    z_step(1)
    z_step(2)
    arrived(relay[0])
    near = forward(0, (0,))
    arrived(direct[1])
    relay.append(relay_weights(1))
    join(0, (0,), near)
    a0 = sums_across(0, (0,))
    z_step(3)
    for copy in relay[1]:
        left(copy)
    direct += [send_weights(k) for k in range(2, n)]
    arrived([moving[key] for key in moving if key[0] == 3])
    near = forward(0, (1,))
    arrived(relay[1])
    join(0, (1,), near)
    left(a0)
    b0 = sums_across(0, (1,))
    near = forward(1, (0, 1))
    lax.fori_loop(0, 16, turn, 0)
    join(1, (0, 1), near)
    left(b0)
    sums = [None, sums_across(1, (0, 1))]
    arrived((a0, b0))
    cot_in.wait()
    own = [middle(0)]
    for k in range(2, n):
        arrived(direct[k])
        relay.append(relay_weights(k))
    grads, passed, out, on = [], [], [], []
    for k in range(n - 2):
        left(sums[k + 1])
        grads.append(grads_across(k, (0, 1)))
        arrived(relay[k + 2])
        near = forward(k + 2, (0, 1))
        sums[k + 1].wait_recv()
        own.append(middle(k + 1))
        join(k + 2, (0, 1), near)
        left(grads[k])
        sums.append(sums_across(k + 2, (0, 1)))
        grads[k].wait_recv()
        passed.append(pass_on(k, (0, 1)))
        if k:
            on.append(sums_on(k - 1, *out[k - 1][:2]))
        arrived((own[k], passed[k]))
        out.append(sums_out(k))
    p, l = n - 2, n - 1
    most, every = tuple(range(n - 1)), tuple(range(n))
    left(sums[l])
    grads.append(grads_across(p, (0, 1)))
    sums[l].wait_recv()
    own.append(middle(l))
    on.append(sums_on(p - 1, *out[p - 1][:2]))
    arrived((own[p], own[l]))
    back(xh, 1, every, False)
    z_sum(0, 0)
    back(xh, 0, every, False)
    left(grads[p])
    far = grads_across(l, (1,))
    grads[p].wait_recv()
    passed.append(pass_on(p, (0, 1)))
    z_sum(0, 1)
    left(far)
    near = grads_across(l, (0,))
    passed[p].wait_recv()
    out.append(sums_out(p))
    z_sum(0, 2)
    far.wait_recv()
    far = pass_on(l, (1,))
    back(1 - xh, 1, most, False)
    far.wait_recv()
    back(1 - xh, 1, (l,), True)
    z_sum(1, 0)
    near.wait_recv()
    near = pass_on(l, (0,))
    back(1 - xh, 0, most, False)
    on.append(sums_on(p, *out[p][:2]))
    z_sum(1, 1)
    z_sum(0, 3)
    near.wait_recv()
    back(1 - xh, 0, (l,), True)
    out.append(sums_direct(l))
    z_sum(1, 2)
    for k in range(p):
        sums_in(k, (*out[k][2:], *on[k]))
    z_sum(1, 3)
    end0 = z_last(0)
    end1 = z_last(1)
    sums_in(p, (*out[p][2:], *on[p]))
    sums_in(l, out[l], True)
    arrived(end0)
    arrived(end1)
    for a in range(2):
        for b in range(2):
            total = (tr[a, b, 0].astype(F32) + tr[a, b, 1].astype(F32)).astype(BF16)
            for i in range(4):
                at = ((a * 4 + i) * 2 + b) * 256
                rows_out[:, at : at + 256] = total[:, i * 256 : (i + 1) * 256]
    for copy in sent:
        copy.wait_send()


def hand_over(*refs):
    n = len(refs) // 3
    here = refs[2 * n : 3 * n]
    into = [pltpu.make_async_copy(refs[i], here[i], refs[-1].at[i]) for i in range(n)]
    out = [pltpu.make_async_copy(here[i], refs[n + i], refs[-1].at[n + i]) for i in range(n)]
    for copy in into:
        copy.start()
    for i in range(n):
        into[i].wait()
        out[i].start()
    for copy in out:
        copy.wait()


def body(tokens, gate_weight, up_weight, cotangent):
    wides = [2 * wide for _, wide in CHUNKS]
    n = len(CHUNKS)
    dma = pltpu.SemaphoreType.DMA

    def per_chunk(*lead, dtype=BF16):
        return [pltpu.VMEM((*lead, wide), dtype) for wide in wides]

    vmem = pl.BlockSpec(memory_space=pltpu.VMEM)
    grid = pl.BlockSpec(memory_space=pl.ANY)
    tile = jax.ShapeDtypeStruct(gate_weight.shape, BF16)
    outs = pl.pallas_call(
        kernel,
        out_shape=(tile, jax.ShapeDtypeStruct(tokens.shape, BF16), tile, tile),
        in_specs=[vmem, grid, grid, grid],
        out_specs=(vmem, vmem, vmem, vmem),
        scratch_shapes=[
            *per_chunk(4, 256),
            *per_chunk(2, 2, 128),
            *per_chunk(2, 2, 128),
            *per_chunk(2, 128),
            *per_chunk(2, 128),
            *per_chunk(2, 2, 128, dtype=F32),
            *per_chunk(2, 2, 2, 128),
            *per_chunk(4, 256),
            *per_chunk(2, 256),
            *per_chunk(2, 128),
            pltpu.VMEM((2, 2, 2, 2, 4, 16, 1024), BF16),
            pltpu.VMEM((1024, 1024), BF16),
            pltpu.VMEM((4, 16, 1024), BF16),
            pltpu.VMEM(gate_weight.shape, BF16),
            pltpu.VMEM((2, 2, 2, 2, 4, 16, 1024), F32),
            pltpu.VMEM((2, 2, STEPS, 2, 2, 16, 1024), BF16),
            pltpu.VMEM((2, 2, STEPS, 2, 2, 16, 1024), BF16),
            pltpu.VMEM((2, 2, 2, 16, 1024), BF16),
            pltpu.VMEM((2, 2, 2, 16, 1024), BF16),
            dma((2 * n + 1,)), dma((7,)), dma((7,)),
            dma((4, 4, 2)), dma((4, 4, 2)),
            dma((n, 4)), dma((n, 4)),
            dma((n, 9)), dma((n, 9)),
            dma((n, 6)), dma((n, 6)),
            dma((2, STEPS, 2, 2)), dma((2, STEPS, 2, 2)),
            dma((7,)), dma((7,)),
        ],
        compiler_params=pltpu.CompilerParams(
            collective_id=0, has_side_effects=True, vmem_limit_bytes=56 * 2**20
        ),
        name="swiglu",
    )(tokens, gate_weight, up_weight, cotangent)
    return pl.pallas_call(
        hand_over,
        out_shape=tuple(jax.ShapeDtypeStruct(a.shape, a.dtype) for a in outs),
        in_specs=[grid] * len(outs),
        out_specs=(grid,) * len(outs),
        scratch_shapes=[*(pltpu.VMEM(a.shape, a.dtype) for a in outs), dma((2 * len(outs),))],
        name="hand_over",
    )(*outs)


def solution(mesh):
    torus = Mesh(mesh.devices.reshape(2, 4, 2, 2, 8), (*DP, *TENSOR))
    specs = (ROWS, BLOCK, BLOCK, BLOCK)
    outs = (BLOCK, ROWS, BLOCK, BLOCK)
    return jax.shard_map(body, mesh=torus, in_specs=specs, out_specs=outs, check_vma=False)
```
